32 devices in a mesh: groups: 2 (over x), seq: 16 (over z, y, core).
Axes of the slice: x: 2, y: 2, z: 4, core: 2. Of those that a mesh axis runs over, the one named last changes fastest.
Arguments:
- frames_in: bfloat16 [4096, 1024], P(('groups', 'seq')), parts along dimension 0, may hold values from -6 to 6
- query_proj: bfloat16 [4096, 512], P(('groups', 'seq')), parts along dimension 0, may hold values from -6 to 6
- key_proj: bfloat16 [4096, 512], P(('groups', 'seq')), parts along dimension 0, may hold values from -6 to 6
- value_proj: bfloat16 [4096, 512], P(('groups', 'seq')), parts along dimension 0, may hold values from -6 to 6
- utterance_lengths: int32 [32], P('groups'), parts along dimension 0, may hold values from 1 to 256, 2048 in all
- bucket_table: int32 [767], replicated, may hold values from 0 to 31
- bucket_bias: float32 [32, 8], replicated, may hold values from -4 to 4
- out_weight: bfloat16 [512, 1024], replicated, may hold values from -0.25 to 0.25
- norm_gain: float32 [1024], replicated, may hold values from 0.1 to 1.9
- expand_weight: bfloat16 [1024, 2048], replicated, may hold values from -0.1875 to 0.1875
- depth_taps: float32 [31, 1024], replicated, may hold values from -1 to 1
- inner_gain: float32 [1024], replicated, may hold values from 0.1 to 1.9
- shrink_weight: bfloat16 [1024, 1024], replicated, may hold values from -0.1875 to 0.1875
Outputs:
- block_out: bfloat16 [4096, 1024], P(('groups', 'seq')), parts along dimension 0
The draws below stay inside these ranges and needn't reach their ends.
There are 2 independent parts, one for each index of `groups`. The reference program is written for one: setup_inputs(seed, part) draws one part's arguments, and reference() takes and returns one part's arrays. A program takes and returns all parts, laid end to end along the dimension named above; an argument that names none is the same for every part. Nothing has to cross between parts.
Inputs may be any that keep to these rules, and one draw needn't show every extreme that they name: `utterance_lengths`: they sum to 2048, and one is exactly 256.
All inputs are finite; a program needn't handle non-finite values.
Results may differ from the reference program's by a relative error of at most 0.014.
Values may be sent and summed in bfloat16 or wider, within the bound.
A program may use at most 64 MiB of HBM per device.

```python
import math
import jax
import jax.numpy as jnp
import numpy as np
from jax import lax

D = 1024
HEADS = 8
HEAD_DIM = 64
KERNEL = 31
DILATION = 4
NB = 32
REACH = 2
ROWS = 128
FRAMES = 2048
UTT_MAX = 256
NUTT = 16
NREL = 767
N_SEQ = 16


def draw_frames_in(key, part):
    base_key = jax.random.fold_in(key, 21)
    row_key = jax.random.fold_in(key, 22)
    col_key = jax.random.fold_in(key, 23)
    row_scale = jnp.exp(jax.random.uniform(row_key, (FRAMES, 1), jnp.float32, math.log(0.3), math.log(3.0)))
    col_scale = jnp.exp(jax.random.uniform(col_key, (1, D), jnp.float32, math.log(0.3), math.log(3.0)))
    base_draw = jax.random.normal(base_key, (FRAMES, D), jnp.float32)
    values = base_draw * row_scale * col_scale
    return jnp.clip(values, -6.0, 6.0).astype(jnp.bfloat16)


def drawn_pair(key):
    width_all = HEADS * HEAD_DIM
    query_key = jax.random.fold_in(key, 31)
    key_key = jax.random.fold_in(key, 32)
    query_out = jnp.clip(1.4 * jax.random.normal(query_key, (FRAMES, width_all), jnp.float32), -6.0, 6.0)
    key_out = jnp.clip(1.4 * jax.random.normal(key_key, (FRAMES, width_all), jnp.float32), -6.0, 6.0)
    return (query_out, key_out)


def draw_query_proj(key, part):
    return drawn_pair(key)[0].astype(jnp.bfloat16)


def draw_key_proj(key, part):
    return drawn_pair(key)[1].astype(jnp.bfloat16)


def touch_ends(result, key, low, largest):
    place = [jax.random.randint(jax.random.fold_in(key, axis), (), 0, length) for axis, length in enumerate(result.shape)]
    main_axis = result.shape.index(max(result.shape))
    next_to = place[:main_axis] + [(place[main_axis] + 1) % result.shape[main_axis]] + place[main_axis + 1:]
    return result.at[tuple(place)].set(low).at[tuple(next_to)].set(largest)


def levels(own_key, dims, shards, low, high):
    loudness = 1.0
    for axis_at, shards_of in shards:
        heights = jax.random.uniform(jax.random.fold_in(jax.random.fold_in(own_key, 6), axis_at), (shards_of,), jnp.float32, low / len(shards), high / len(shards))
        loudness = loudness * jnp.repeat(jnp.exp(heights), dims[axis_at] // shards_of).reshape((-1,) + (1,) * (len(dims) - 1 - axis_at))
    return loudness


def length_profile(number_of, total, bound, slope):
    portions = [(1 << 20) // math.isqrt(rank ** slope) + 1 for rank in range(2, number_of + 1)]
    rest, counts = total - bound - (number_of - 1), [1] * (number_of - 1)
    while rest > 0:
        free = [i for i in range(number_of - 1) if counts[i] < bound]
        mass, budget = sum([portions[i] for i in free]), rest
        for i in free:
            extra = min(bound - counts[i], max(1, budget * portions[i] // mass), rest)
            counts[i] = counts[i] + extra
            rest = rest - extra
    return np.array([bound] + counts)


def ragged(own_key, number_of, total, reach, slope):
    if number_of == 2:
        one = jax.random.randint(own_key, (), max(1, total - reach), min(reach, total - 1) + 1)
        return jnp.stack([one, total - one])
    lengths = jnp.asarray(length_profile(number_of, total, reach, slope), jnp.int32)
    pairs = (number_of - 1) // 2
    giver, taker = lengths[1:1 + 2 * pairs:2], lengths[2:2 + 2 * pairs:2]
    room = jnp.minimum(giver - 1, reach - taker)
    moved = jax.random.randint(jax.random.fold_in(own_key, 1), (pairs,), 0, 1 << 20) % (room + 1)
    lengths = lengths.at[1:1 + 2 * pairs:2].set(giver - moved).at[2:2 + 2 * pairs:2].set(taker + moved)
    return lengths[jax.random.permutation(jax.random.fold_in(own_key, 2), number_of)]


def normal_values(stream_key, extent, width, reach, split=(), kind=jnp.bfloat16):
    loudness = levels(stream_key, extent, split, -0.22, 0.18) if split else 1.0
    values = jax.random.normal(stream_key, extent, jnp.float32) * width * loudness
    return jnp.minimum(jnp.maximum(values, -reach), reach).astype(kind)


def setup_inputs(seed: int = 0, part: int = 0) -> dict:
    splits = jax.random.split(jax.random.key(seed), 14)
    part_splits = jax.random.split(jax.random.fold_in(splits[13], part), 14)
    frames_in = draw_frames_in(jax.random.fold_in(jax.random.fold_in(splits[13], part), 71), part)
    query_proj = draw_query_proj(jax.random.fold_in(jax.random.fold_in(splits[13], part), 71), part)
    key_proj = draw_key_proj(jax.random.fold_in(jax.random.fold_in(splits[13], part), 71), part)
    value_proj = normal_values(part_splits[3], (FRAMES, HEADS * HEAD_DIM), 1.0, 6.0, ((0, 16),))
    utterance_lengths = ragged(part_splits[4], NUTT, FRAMES, UTT_MAX, 2).astype(jnp.int32)
    bucket_table = touch_ends(jax.random.randint(splits[5], (NREL,), 0, NB), jax.random.fold_in(splits[5], 1), 0, NB - 1).astype(jnp.int32)
    bucket_bias = normal_values(splits[6], (NB, HEADS), 1.0, 4.0, (), jnp.float32)
    out_weight = normal_values(splits[7], (HEADS * HEAD_DIM, D), (HEADS * HEAD_DIM) ** -0.5, 0.25)
    norm_gain = jnp.clip(1.0 + 0.18 * jax.random.normal(splits[8], (D,), jnp.float32), 0.1, 1.9)
    expand_weight = normal_values(splits[9], (D, 2 * D), D ** -0.5, 0.1875)
    depth_taps = normal_values(splits[10], (KERNEL, D), KERNEL ** -0.5, 1.0, (), jnp.float32)
    inner_gain = jnp.clip(1.0 + 0.18 * jax.random.normal(splits[11], (D,), jnp.float32), 0.1, 1.9)
    shrink_weight = normal_values(splits[12], (D, D), D ** -0.5, 0.1875)
    return {"frames_in": frames_in, "query_proj": query_proj, "key_proj": key_proj, "value_proj": value_proj, "utterance_lengths": utterance_lengths, "bucket_table": bucket_table, "bucket_bias": bucket_bias, "out_weight": out_weight, "norm_gain": norm_gain, "expand_weight": expand_weight, "depth_taps": depth_taps, "inner_gain": inner_gain, "shrink_weight": shrink_weight}


norm_epsilon = 1e-05
masked_score = -1e+30

def segment_of(positions, bounds):
    inside = lax.optimization_barrier(jnp.sum((positions[:, None] >= bounds[None, :]).astype(jnp.int32), axis=1))
    return jnp.where(positions < 0, -1, inside).astype(jnp.int32)

def layer_norm(values, gain_vec):
    row_mean = lax.optimization_barrier(jnp.mean(values, axis=-1, keepdims=True))
    centred = values - row_mean
    spread = lax.optimization_barrier(jnp.mean(centred * centred, axis=-1, keepdims=True))
    return centred * lax.rsqrt(spread + norm_epsilon) * gain_vec

def gated_units(mid, norm_gain, expand_weight):
    model_width = mid.shape[1]
    normed = layer_norm(mid.astype(jnp.float32), norm_gain).astype(jnp.bfloat16)
    hidden = jnp.dot(normed, expand_weight, preferred_element_type=jnp.float32)
    return (hidden[:, :model_width] * jax.nn.sigmoid(hidden[:, model_width:])).astype(jnp.bfloat16)

def reference(frames_in, query_proj, key_proj, value_proj, utterance_lengths, bucket_table, bucket_bias, out_weight, norm_gain, expand_weight, depth_taps, inner_gain, shrink_weight):
    total_rows = ROWS * N_SEQ
    att_width = HEADS * HEAD_DIM
    bounds = jnp.cumsum(utterance_lengths).astype(jnp.int32)
    segments = segment_of(jnp.arange(total_rows, dtype=jnp.int32), bounds)
    margin = REACH * ROWS
    window_rows = (2 * REACH + 1) * ROWS
    key_pad = jnp.pad(key_proj, ((margin, margin), (0, 0)))
    value_pad = jnp.pad(value_proj, ((margin, margin), (0, 0)))
    segment_pad = jnp.pad(segments, (margin, margin), constant_values=-1)
    bias_line = bucket_bias[bucket_table].T
    rel_index = (jnp.arange(window_rows, dtype=jnp.int32)[None, :] - jnp.arange(ROWS, dtype=jnp.int32)[:, None] + ROWS - 1).astype(jnp.int32)
    block_bias = bias_line[:, rel_index]
    scaling = HEAD_DIM ** (-0.5)

    def one_block(block_index):
        first_row = (block_index * ROWS).astype(jnp.int32)
        queries = lax.dynamic_slice_in_dim(query_proj, first_row, ROWS, 0).astype(jnp.float32).reshape(ROWS, HEADS, HEAD_DIM)
        keys_here = lax.dynamic_slice_in_dim(key_pad, first_row, window_rows, 0).astype(jnp.float32).reshape(window_rows, HEADS, HEAD_DIM)
        values_here = lax.dynamic_slice_in_dim(value_pad, first_row, window_rows, 0).astype(jnp.float32).reshape(window_rows, HEADS, HEAD_DIM)
        query_segment = lax.dynamic_slice_in_dim(segments, first_row, ROWS, 0)
        key_segment = lax.dynamic_slice_in_dim(segment_pad, first_row, window_rows, 0)
        scores = jnp.einsum('rhd,chd->hrc', queries, keys_here) * scaling + block_bias
        same_utterance = (query_segment[:, None] == key_segment[None, :])[None]
        scores = jnp.where(same_utterance, scores, masked_score)
        row_max = lax.optimization_barrier(jnp.max(scores, axis=2, keepdims=True))
        weights = jnp.exp(scores - row_max)
        row_total = lax.optimization_barrier(jnp.sum(weights, axis=2))
        rounded = lax.optimization_barrier(weights.astype(jnp.bfloat16)).astype(jnp.float32)
        weighted = jnp.einsum('hrc,chd->rhd', rounded, values_here)
        return (weighted / row_total.T[:, :, None]).astype(jnp.bfloat16).reshape(ROWS, att_width)
    attended = lax.map(one_block, jnp.arange(N_SEQ, dtype=jnp.int32)).reshape(total_rows, att_width)
    mid = (frames_in.astype(jnp.float32) + jnp.dot(attended, out_weight, preferred_element_type=jnp.float32)).astype(jnp.bfloat16)
    gated = gated_units(mid, norm_gain, expand_weight)
    halo_rows = DILATION * (KERNEL - 1) // 2
    widened = jnp.pad(gated, ((halo_rows, halo_rows), (0, 0))).astype(jnp.float32)
    conv_sum = jnp.zeros((total_rows, D), jnp.float32)
    for tap_index in range(KERNEL):
        conv_sum = conv_sum + depth_taps[tap_index] * widened[DILATION * tap_index:DILATION * tap_index + total_rows]
    inner_normed = layer_norm(conv_sum, inner_gain)
    activated = (inner_normed * jax.nn.sigmoid(inner_normed)).astype(jnp.bfloat16)
    return (mid.astype(jnp.float32) + jnp.dot(activated, shrink_weight, preferred_element_type=jnp.float32)).astype(jnp.bfloat16)
```

```python
import functools

import jax
import jax.numpy as jnp
from jax import lax
from jax.experimental import pallas as pl
from jax.experimental.pallas import tpu as pltpu
from jax.sharding import PartitionSpec as P

KERNEL = 31
DILATION = 4
REACH = 2
SLOTS = 2 * REACH + 1
CHUNK = 128
GATE_COLS = 256
HALO = 64
CONV_ROWS = 32
CONV_COLS = 512

norm_epsilon = 1e-05
masked_score = -1e30


def layer_norm(values, gain_vec):
    row_mean = jnp.mean(values, axis=-1, keepdims=True)
    centred = values - row_mean
    spread = jnp.mean(centred * centred, axis=-1, keepdims=True)
    return centred * lax.rsqrt(spread + norm_epsilon) * gain_vec


def kernel(
    seq_count,
    lengths,
    table,
    bucket_bias,
    norm_gain,
    inner_gain,
    frames_hbm,
    query_hbm,
    key_hbm,
    value_hbm,
    out_w_hbm,
    expand_hbm,
    taps_hbm,
    shrink_hbm,
    out,
    frames,
    query,
    out_w,
    expand,
    taps,
    shrink,
    kv,
    table_pad,
    bias,
    attended,
    gated,
    plain,
    offset4,
    conv,
    local_sem,
    own_sem,
    p_send,
    p_recv,
    y_send,
    y_recv,
    z_send,
    z_recv,
    c_send,
    c_recv,
    h_send,
    h_recv,
):
    rows, width = frames.shape
    att_width = query.shape[1]
    chunks = att_width // CHUNK
    head_width = att_width // bucket_bias.shape[1]
    window = SLOTS * rows
    gate_chunks = width // GATE_COLS

    me = lax.axis_index("seq")
    core = lax.rem(me, 2)
    is_a = lax.rem(me, 4) < 2
    outer = is_a == (core == 0)
    partner = me + 1 - 2 * core
    y_peer = jnp.where(is_a, me + 2, me - 2)
    z_to = jnp.where(is_a, me + 4, me - 4)
    z_from = jnp.where(is_a, me - 4, me + 4)
    beside = jnp.where(core == 0, me - 1, me + 1)
    z_sends = jnp.logical_and(z_to >= 0, z_to < seq_count)
    z_gets = jnp.logical_and(z_from >= 0, z_from < seq_count)
    beside_is = jnp.logical_and(beside >= 0, beside < seq_count)
    c_sends = jnp.logical_or(outer, z_gets)
    c_gets = jnp.logical_or(jnp.logical_not(outer), z_gets)
    y_slot = jnp.where(is_a, 4, 0)
    z_slot = jnp.where(is_a, 0, 4)
    c_slot = jnp.where(core == 0, 1, 3)

    def slot_rows(slot):
        return pl.ds(pl.multiple_of(slot * rows, rows), rows)

    own = []
    for part, source in enumerate((key_hbm, value_hbm)):
        for g in range(chunks):
            own.append(
                pltpu.make_async_copy(
                    source.at[:, pl.ds(g * CHUNK, CHUNK)],
                    kv.at[g, part, pl.ds(REACH * rows, rows), :],
                    own_sem.at[g, part],
                )
            )
    local = [
        pltpu.make_async_copy(source, target, local_sem.at[i])
        for i, (source, target) in enumerate(
            (
                (query_hbm, query),
                (frames_hbm, frames),
                (out_w_hbm, out_w),
                (expand_hbm, expand),
                (taps_hbm, taps),
                (shrink_hbm, shrink),
            )
        )
    ]

    barrier = pltpu.get_barrier_semaphore()

    def greet(device):
        pl.semaphore_signal(
            barrier, inc=1, device_id={"seq": device}, device_id_type=pl.DeviceIdType.MESH
        )

    greet(partner)
    greet(y_peer)
    pl.when(z_sends)(lambda: greet(z_to))
    pl.when(z_gets)(lambda: greet(z_from))
    pl.when(beside_is)(lambda: greet(beside))
    for copy in own:
        copy.start()
    local[0].start()
    greetings = (
        2 + z_sends.astype(jnp.int32) + z_gets.astype(jnp.int32) + beside_is.astype(jnp.int32)
    )
    pl.semaphore_wait(barrier, greetings)

    def remote(source, target, send, recv, device):
        return pltpu.make_async_remote_copy(
            src_ref=source,
            dst_ref=target,
            send_sem=send,
            recv_sem=recv,
            device_id={"seq": device},
            device_id_type=pl.DeviceIdType.MESH,
        )

    def own_copy(g, part, slot, send, recv, device):
        source = (key_hbm, value_hbm)[part]
        return remote(
            source.at[:, pl.ds(g * CHUNK, CHUNK)],
            kv.at[g, part, slot_rows(slot), :],
            send.at[g, part],
            recv.at[g, part],
            device,
        )

    def relay(g, from_slot, to_slot, send, recv, device):
        return remote(
            kv.at[g, :, slot_rows(from_slot), :],
            kv.at[g, :, slot_rows(to_slot), :],
            send.at[g],
            recv.at[g],
            device,
        )

    def y_copy(g, part, slot):
        return own_copy(g, part, slot, y_send, y_recv, y_peer)

    def p_copy(g, part, slot):
        return own_copy(g, part, slot, p_send, p_recv, partner)

    y_target = jnp.where(is_a, 0, 4)
    p_target = 2 * core + 1
    p_slot = 3 - 2 * core
    c_target = jnp.where(core == 0, 3, 1)
    c_source = jnp.where(outer, y_slot, z_slot)

    def z_copy(g):
        return relay(g, y_slot, z_slot, z_send, z_recv, z_to)

    def c_copy(g, target):
        return relay(g, c_source, target, c_send, c_recv, partner)

    for g in range(chunks):
        for part in range(2):
            y_copy(g, part, y_target).start()
        for part in range(2):
            p_copy(g, part, p_target).start()
    for copy in local[1:]:
        copy.start()

    @pl.when(jnp.logical_not(z_gets))
    def _():
        for g in range(chunks):
            kv[g, :, slot_rows(z_slot), :] = jnp.zeros((2, rows, CHUNK), kv.dtype)

    @pl.when(jnp.logical_not(c_gets))
    def _():
        for g in range(chunks):
            kv[g, :, slot_rows(c_slot), :] = jnp.zeros((2, rows, CHUNK), kv.dtype)

    zero_halo = jnp.zeros((HALO, width), gated.dtype)

    @pl.when(me == 0)
    def _():
        gated[0:HALO, :] = zero_halo

    @pl.when(me == seq_count - 1)
    def _():
        gated[HALO + rows : 2 * HALO + rows, :] = zero_halo

    query_at = me * rows + lax.broadcasted_iota(jnp.int32, (rows, 1), 0)
    key_at = (me - REACH) * rows + lax.broadcasted_iota(jnp.int32, (1, window), 1)

    def count(u, state):
        bound, query_seg, key_seg = state
        bound = bound + lengths[u]
        return (
            bound,
            query_seg + (query_at >= bound).astype(jnp.int32),
            key_seg + (key_at >= bound).astype(jnp.int32),
        )

    utterances = lengths.shape[0]
    _, query_seg, key_seg = lax.fori_loop(
        0,
        utterances,
        count,
        (jnp.int32(0), jnp.zeros((rows, 1), jnp.int32), jnp.zeros((1, window), jnp.int32)),
        unroll=utterances <= 32,
    )
    key_seg = jnp.where(key_at < 0, -1, key_seg)

    line_length = table.shape[1]
    padded_length = window + rows
    table_pad[...] = jnp.zeros_like(table_pad)
    table_pad[:, 0:line_length] = table[...]
    buckets = bucket_bias.shape[0]
    hits = (
        lax.broadcasted_iota(jnp.int32, (buckets, padded_length), 0) == table_pad[...]
    ).astype(jnp.float32)
    bias_line = lax.dot_general(
        bucket_bias[...],
        hits,
        (((0,), (0,)), ((), ())),
        precision=lax.Precision.HIGHEST,
        preferred_element_type=jnp.float32,
    )
    heads_here = CHUNK // head_width

    def make_bias(g):
        same = query_seg == key_seg
        for h in range(heads_here):
            head = g * heads_here + h
            line = jnp.broadcast_to(bias_line[head : head + 1, :], (rows, padded_length))
            skewed = pltpu.roll(line, padded_length - (rows - 1), 1, stride=1, stride_axis=0)
            bias[g, h * rows : (h + 1) * rows, :] = jnp.where(
                same, skewed[:, :window], masked_score
            )

    head_of_lane = lax.broadcasted_iota(jnp.int32, (rows, CHUNK), 1) // head_width

    def attend(g):
        for part in range(2):
            own[part * chunks + g].wait()
            p_copy(g, part, p_slot).wait_recv()

        @pl.when(c_gets)
        def _():
            c_copy(g, c_slot).wait_recv()

        chunk_query = query[:, g * CHUNK : (g + 1) * CHUNK]
        stacked = jnp.concatenate(
            [
                jnp.where(head_of_lane == h, chunk_query, jnp.zeros_like(chunk_query))
                for h in range(heads_here)
            ],
            axis=0,
        )
        scores = lax.dot_general(
            stacked, kv[g, 0], (((1,), (1,)), ((), ())), preferred_element_type=jnp.float32
        )
        scores = scores * (head_width**-0.5) + bias[g]
        top = jnp.max(scores, axis=1, keepdims=True)
        weights = jnp.exp(scores - top)
        row_total = jnp.sum(weights, axis=1, keepdims=True)
        weighted = jnp.dot(
            weights.astype(jnp.bfloat16), kv[g, 1], preferred_element_type=jnp.float32
        )
        normal = (weighted / row_total).astype(jnp.bfloat16)
        result = normal[0:rows]
        for h in range(1, heads_here):
            result = jnp.where(head_of_lane == h, normal[h * rows : (h + 1) * rows], result)
        attended[:, g * CHUNK : (g + 1) * CHUNK] = result

    def pass_z(g):
        @pl.when(z_gets)
        def _():
            relay(g, y_slot, z_slot, z_send, z_recv, z_to).wait_recv()

        @pl.when(jnp.logical_and(z_gets, jnp.logical_not(outer)))
        def _():
            c_copy(g, c_target).start()

    local[0].wait()
    for g in range(chunks):
        make_bias(g)
        for part in range(2):
            y_copy(g, part, y_slot).wait_recv()
        pl.when(z_sends)(lambda g=g: z_copy(g).start())
        pl.when(outer)(lambda g=g: c_copy(g, c_target).start())
        if g >= 1:
            pass_z(g - 1)
        if g >= 2:
            attend(g - 2)
    pass_z(chunks - 1)
    for g in range(max(0, chunks - 2), chunks):
        attend(g)

    local[1].wait()
    local[2].wait()
    mid = (
        frames[...].astype(jnp.float32)
        + jnp.dot(attended[...], out_w[...], preferred_element_type=jnp.float32)
    ).astype(jnp.bfloat16)
    frames[...] = mid
    normed = layer_norm(mid.astype(jnp.float32), norm_gain[...]).astype(jnp.bfloat16)
    local[3].wait()

    def to_prev(j):
        cols = pl.ds(j * GATE_COLS, GATE_COLS)
        return remote(
            gated.at[pl.ds(HALO, HALO), cols],
            gated.at[pl.ds(HALO + rows, HALO), cols],
            h_send.at[0, j],
            h_recv.at[0, j],
            me - 1,
        )

    def to_next(j):
        cols = pl.ds(j * GATE_COLS, GATE_COLS)
        return remote(
            gated.at[pl.ds(rows, HALO), cols],
            gated.at[pl.ds(0, HALO), cols],
            h_send.at[1, j],
            h_recv.at[1, j],
            me + 1,
        )

    has_prev = me > 0
    has_next = me < seq_count - 1
    for j in range(gate_chunks):
        first = j * GATE_COLS
        cols = slice(first, first + GATE_COLS)
        linear = jnp.dot(normed, expand[:, cols], preferred_element_type=jnp.float32)
        gate = jnp.dot(
            normed,
            expand[:, width + first : width + first + GATE_COLS],
            preferred_element_type=jnp.float32,
        )
        units = (linear * jax.nn.sigmoid(gate)).astype(jnp.bfloat16)
        gated[HALO : HALO + rows, cols] = units
        pl.when(has_prev)(lambda j=j: to_prev(j).start())
        pl.when(has_next)(lambda j=j: to_next(j).start())
        wide = units.astype(jnp.float32)
        plain[HALO : HALO + rows, cols] = wide
        offset4[HALO - 4 : HALO - 4 + rows, cols] = wide

    local[4].wait()

    def first_row(i, t):
        return i * CONV_ROWS + HALO + DILATION * (t - KERNEL // 2)

    def is_own(i, t):
        return first_row(i, t) >= HALO and first_row(i, t) + CONV_ROWS <= HALO + rows

    def add_taps(total, i, cols, chosen):
        for t in chosen:
            row = first_row(i, t)
            source = plain if row % 8 == 0 else offset4
            row -= row % 8
            term = taps[t : t + 1, cols] * source[row : row + CONV_ROWS, cols]
            total = term if total is None else total + term
        return total

    tiles = [
        (i, slice(c * CONV_COLS, (c + 1) * CONV_COLS))
        for c in range(width // CONV_COLS)
        for i in range(rows // CONV_ROWS)
    ]
    for i, cols in tiles:
        conv[i * CONV_ROWS : (i + 1) * CONV_ROWS, cols] = add_taps(
            None, i, cols, [t for t in range(KERNEL) if is_own(i, t)]
        )

    for j in range(gate_chunks):
        pl.when(has_next)(lambda j=j: to_prev(j).wait_recv())
        pl.when(has_prev)(lambda j=j: to_next(j).wait_recv())
    left = gated[0:HALO, :].astype(jnp.float32)
    right = gated[HALO + rows : 2 * HALO + rows, :].astype(jnp.float32)
    plain[0:HALO, :] = left
    plain[HALO + rows : 2 * HALO + rows, :] = right
    offset4[0 : HALO - 4, :] = left[4:HALO]
    offset4[HALO - 4 + rows : 2 * HALO - 4 + rows, :] = right
    for i, cols in tiles:
        here = slice(i * CONV_ROWS, (i + 1) * CONV_ROWS)
        conv[here, cols] = add_taps(
            conv[here, cols], i, cols, [t for t in range(KERNEL) if not is_own(i, t)]
        )

    inner = layer_norm(conv[...], inner_gain[...])
    activated = (inner * jax.nn.sigmoid(inner)).astype(jnp.bfloat16)
    local[5].wait()
    out[...] = (
        frames[...].astype(jnp.float32)
        + jnp.dot(activated, shrink[...], preferred_element_type=jnp.float32)
    ).astype(jnp.bfloat16)

    for g in range(chunks):
        for part in range(2):
            y_copy(g, part, y_target).wait_send()
            p_copy(g, part, p_target).wait_send()
        pl.when(z_sends)(lambda g=g: z_copy(g).wait_send())
        pl.when(c_sends)(lambda g=g: c_copy(g, c_target).wait_send())
    for j in range(gate_chunks):
        pl.when(has_prev)(lambda j=j: to_prev(j).wait_send())
        pl.when(has_next)(lambda j=j: to_next(j).wait_send())


def on_device(
    frames_in,
    query_proj,
    key_proj,
    value_proj,
    utterance_lengths,
    bucket_table,
    bucket_bias,
    out_weight,
    norm_gain,
    expand_weight,
    depth_taps,
    inner_gain,
    shrink_weight,
):
    rows, width = frames_in.shape
    att_width = query_proj.shape[1]
    chunks = att_width // CHUNK
    gate_chunks = width // GATE_COLS
    window = SLOTS * rows
    heads_here = CHUNK // (att_width // bucket_bias.shape[1])
    wide_rows = rows + 2 * HALO
    bf16, f32 = jnp.bfloat16, jnp.float32
    vmem = pl.BlockSpec(memory_space=pltpu.VMEM)
    anywhere = pl.BlockSpec(memory_space=pl.ANY)
    dma = pltpu.SemaphoreType.DMA
    return pl.pallas_call(
        functools.partial(kernel, lax.axis_size("seq")),
        out_shape=jax.ShapeDtypeStruct((rows, width), bf16),
        in_specs=[pl.BlockSpec(memory_space=pltpu.SMEM)] + [vmem] * 4 + [anywhere] * 8,
        out_specs=vmem,
        scratch_shapes=[
            pltpu.VMEM((rows, width), bf16),
            pltpu.VMEM((rows, att_width), bf16),
            pltpu.VMEM(out_weight.shape, bf16),
            pltpu.VMEM(expand_weight.shape, bf16),
            pltpu.VMEM(depth_taps.shape, f32),
            pltpu.VMEM(shrink_weight.shape, bf16),
            pltpu.VMEM((chunks, 2, window, CHUNK), bf16),
            pltpu.VMEM((1, window + rows), jnp.int32),
            pltpu.VMEM((chunks, heads_here * rows, window), f32),
            pltpu.VMEM((rows, att_width), bf16),
            pltpu.VMEM((wide_rows, width), bf16),
            pltpu.VMEM((wide_rows, width), f32),
            pltpu.VMEM((wide_rows, width), f32),
            pltpu.VMEM((rows, width), f32),
            dma((6,)),
            dma((chunks, 2)),
            dma((chunks, 2)),
            dma((chunks, 2)),
            dma((chunks, 2)),
            dma((chunks, 2)),
            dma((chunks,)),
            dma((chunks,)),
            dma((chunks,)),
            dma((chunks,)),
            dma((2, gate_chunks)),
            dma((2, gate_chunks)),
        ],
        compiler_params=pltpu.CompilerParams(
            collective_id=0, has_side_effects=True, vmem_limit_bytes=40 * 1024 * 1024
        ),
    )(
        utterance_lengths,
        bucket_table.reshape(1, -1),
        bucket_bias,
        norm_gain.reshape(1, -1),
        inner_gain.reshape(1, -1),
        frames_in,
        query_proj,
        key_proj,
        value_proj,
        out_weight,
        expand_weight,
        depth_taps,
        shrink_weight,
    )


def solution(mesh):
    placed = (
        P(("groups", "seq"), None),
        P(("groups", "seq"), None),
        P(("groups", "seq"), None),
        P(("groups", "seq"), None),
        P("groups"),
        P(),
        P(),
        P(),
        P(),
        P(),
        P(),
        P(),
        P(),
    )
    return jax.shard_map(
        on_device, mesh=mesh, in_specs=placed, out_specs=P(("groups", "seq"), None), check_vma=False
    )
```

```python
import functools

import jax
import jax.numpy as jnp
from jax import lax
from jax.experimental import pallas as pl
from jax.experimental.pallas import tpu as pltpu
from jax.sharding import PartitionSpec as P

KERNEL = 31
DILATION = 4
REACH = 2
SLOTS = 2 * REACH + 1
CHUNK = 128
GATE_COLS = 256
HALO = 64
CONV_ROWS = 32
CONV_COLS = 512

norm_epsilon = 1e-05
masked_score = -1e30


def layer_norm(values, gain_vec):
    row_mean = jnp.mean(values, axis=-1, keepdims=True)
    centred = values - row_mean
    spread = jnp.mean(centred * centred, axis=-1, keepdims=True)
    return centred * lax.rsqrt(spread + norm_epsilon) * gain_vec


def kernel(
    seq_count,
    lengths_hbm,
    table_hbm,
    bucket_bias_hbm,
    norm_gain_hbm,
    inner_gain_hbm,
    frames_hbm,
    query_hbm,
    key_hbm,
    value_hbm,
    out_w_hbm,
    expand_hbm,
    taps_hbm,
    shrink_hbm,
    out,
    lengths,
    table,
    bucket_bias,
    norm_gain,
    inner_gain,
    frames,
    query,
    out_w,
    expand,
    taps,
    shrink,
    kv,
    table_pad,
    bias,
    attended,
    gated,
    plain,
    offset4,
    conv,
    local_sem,
    own_sem,
    p_send,
    p_recv,
    y_send,
    y_recv,
    z_send,
    z_recv,
    c_send,
    c_recv,
    h_send,
    h_recv,
):
    rows, width = frames.shape
    att_width = query.shape[1]
    chunks = att_width // CHUNK
    head_width = att_width // bucket_bias.shape[0]
    window = SLOTS * rows
    gate_chunks = width // GATE_COLS

    me = lax.axis_index("seq")
    core = lax.rem(me, 2)
    is_a = lax.rem(me, 4) < 2
    outer = is_a == (core == 0)
    partner = me + 1 - 2 * core
    y_peer = jnp.where(is_a, me + 2, me - 2)
    z_to = jnp.where(is_a, me + 4, me - 4)
    z_from = jnp.where(is_a, me - 4, me + 4)
    beside = jnp.where(core == 0, me - 1, me + 1)
    z_sends = jnp.logical_and(z_to >= 0, z_to < seq_count)
    z_gets = jnp.logical_and(z_from >= 0, z_from < seq_count)
    beside_is = jnp.logical_and(beside >= 0, beside < seq_count)
    c_sends = jnp.logical_or(outer, z_gets)
    c_gets = jnp.logical_or(jnp.logical_not(outer), z_gets)
    y_slot = jnp.where(is_a, 4, 0)
    z_slot = jnp.where(is_a, 0, 4)
    c_slot = jnp.where(core == 0, 1, 3)

    def slot_rows(slot):
        return pl.ds(pl.multiple_of(slot * rows, rows), rows)

    own = []
    for part, source in enumerate((key_hbm, value_hbm)):
        for g in range(chunks):
            own.append(
                pltpu.make_async_copy(
                    source.at[:, pl.ds(g * CHUNK, CHUNK)],
                    kv.at[g, part, pl.ds(REACH * rows, rows), :],
                    own_sem.at[g, part],
                )
            )
    local = [
        pltpu.make_async_copy(source, target, local_sem.at[i])
        for i, (source, target) in enumerate(
            (
                (lengths_hbm, lengths),
                (table_hbm, table),
                (bucket_bias_hbm, bucket_bias),
                (query_hbm, query),
                (frames_hbm, frames),
                (out_w_hbm, out_w),
                (norm_gain_hbm, norm_gain),
                (expand_hbm, expand),
                (taps_hbm, taps),
                (inner_gain_hbm, inner_gain),
                (shrink_hbm, shrink),
            )
        )
    ]

    barrier = pltpu.get_barrier_semaphore()

    def greet(device):
        pl.semaphore_signal(
            barrier, inc=1, device_id={"seq": device}, device_id_type=pl.DeviceIdType.MESH
        )

    greet(partner)
    greet(y_peer)
    pl.when(z_sends)(lambda: greet(z_to))
    pl.when(z_gets)(lambda: greet(z_from))
    pl.when(beside_is)(lambda: greet(beside))
    for copy in local[:4] + own:
        copy.start()
    greetings = (
        2 + z_sends.astype(jnp.int32) + z_gets.astype(jnp.int32) + beside_is.astype(jnp.int32)
    )
    pl.semaphore_wait(barrier, greetings)

    def remote(source, target, send, recv, device):
        return pltpu.make_async_remote_copy(
            src_ref=source,
            dst_ref=target,
            send_sem=send,
            recv_sem=recv,
            device_id={"seq": device},
            device_id_type=pl.DeviceIdType.MESH,
        )

    def own_copy(g, part, slot, send, recv, device):
        source = (key_hbm, value_hbm)[part]
        return remote(
            source.at[:, pl.ds(g * CHUNK, CHUNK)],
            kv.at[g, part, slot_rows(slot), :],
            send.at[g, part],
            recv.at[g, part],
            device,
        )

    def relay(g, from_slot, to_slot, send, recv, device):
        return remote(
            kv.at[g, :, slot_rows(from_slot), :],
            kv.at[g, :, slot_rows(to_slot), :],
            send.at[g],
            recv.at[g],
            device,
        )

    def y_copy(g, part, slot):
        return own_copy(g, part, slot, y_send, y_recv, y_peer)

    def p_copy(g, part, slot):
        return own_copy(g, part, slot, p_send, p_recv, partner)

    y_target = jnp.where(is_a, 0, 4)
    p_target = 2 * core + 1
    p_slot = 3 - 2 * core
    c_target = jnp.where(core == 0, 3, 1)
    c_source = jnp.where(outer, y_slot, z_slot)

    def z_copy(g):
        return relay(g, y_slot, z_slot, z_send, z_recv, z_to)

    def c_copy(g, target):
        return relay(g, c_source, target, c_send, c_recv, partner)

    for g in range(chunks):
        for part in range(2):
            y_copy(g, part, y_target).start()
        for part in range(2):
            p_copy(g, part, p_target).start()
    for copy in local[4:]:
        copy.start()

    @pl.when(jnp.logical_not(z_gets))
    def _():
        for g in range(chunks):
            kv[g, :, slot_rows(z_slot), :] = jnp.zeros((2, rows, CHUNK), kv.dtype)

    @pl.when(jnp.logical_not(c_gets))
    def _():
        for g in range(chunks):
            kv[g, :, slot_rows(c_slot), :] = jnp.zeros((2, rows, CHUNK), kv.dtype)

    zero_halo = jnp.zeros((HALO, width), gated.dtype)

    @pl.when(me == 0)
    def _():
        gated[0:HALO, :] = zero_halo

    @pl.when(me == seq_count - 1)
    def _():
        gated[HALO + rows : 2 * HALO + rows, :] = zero_halo

    for copy in local[:3]:
        copy.wait()

    query_at = me * rows + lax.broadcasted_iota(jnp.int32, (rows, 1), 0)
    key_at = (me - REACH) * rows + lax.broadcasted_iota(jnp.int32, (1, window), 1)

    def count(u, state):
        bound, query_seg, key_seg = state
        bound = bound + lengths[u]
        return (
            bound,
            query_seg + (query_at >= bound).astype(jnp.int32),
            key_seg + (key_at >= bound).astype(jnp.int32),
        )

    utterances = lengths.shape[0]
    _, query_seg, key_seg = lax.fori_loop(
        0,
        utterances,
        count,
        (jnp.int32(0), jnp.zeros((rows, 1), jnp.int32), jnp.zeros((1, window), jnp.int32)),
        unroll=utterances <= 32,
    )
    key_seg = jnp.where(key_at < 0, -1, key_seg)

    line_length = table.shape[0]
    padded_length = window + rows
    table_pad[...] = jnp.zeros_like(table_pad)
    table_pad[:, 0:line_length] = table[...].reshape(1, line_length)
    buckets = bucket_bias.shape[1]
    hits = (
        lax.broadcasted_iota(jnp.int32, (buckets, padded_length), 0) == table_pad[...]
    ).astype(jnp.float32)
    bias_line = jnp.dot(
        bucket_bias[...],
        hits,
        precision=lax.Precision.HIGHEST,
        preferred_element_type=jnp.float32,
    )
    heads_here = CHUNK // head_width

    def make_bias(g):
        same = query_seg == key_seg
        for h in range(heads_here):
            head = g * heads_here + h
            line = jnp.broadcast_to(bias_line[head : head + 1, :], (rows, padded_length))
            skewed = pltpu.roll(line, padded_length - (rows - 1), 1, stride=1, stride_axis=0)
            bias[g, h * rows : (h + 1) * rows, :] = jnp.where(
                same, skewed[:, :window], masked_score
            )

    head_of_lane = lax.broadcasted_iota(jnp.int32, (rows, CHUNK), 1) // head_width

    def attend(g):
        for part in range(2):
            own[part * chunks + g].wait()
            p_copy(g, part, p_slot).wait_recv()

        @pl.when(c_gets)
        def _():
            c_copy(g, c_slot).wait_recv()

        chunk_query = query[:, g * CHUNK : (g + 1) * CHUNK]
        stacked = jnp.concatenate(
            [
                jnp.where(head_of_lane == h, chunk_query, jnp.zeros_like(chunk_query))
                for h in range(heads_here)
            ],
            axis=0,
        )
        scores = lax.dot_general(
            stacked, kv[g, 0], (((1,), (1,)), ((), ())), preferred_element_type=jnp.float32
        )
        scores = scores * (head_width**-0.5) + bias[g]
        top = jnp.max(scores, axis=1, keepdims=True)
        weights = jnp.exp(scores - top)
        values_and_ones = jnp.concatenate([kv[g, 1], jnp.ones_like(kv[g, 1])], axis=1)
        weighted = jnp.dot(
            weights.astype(jnp.bfloat16), values_and_ones, preferred_element_type=jnp.float32
        )
        normal = (weighted[:, :CHUNK] / weighted[:, CHUNK:]).astype(jnp.bfloat16)
        result = normal[0:rows]
        for h in range(1, heads_here):
            result = jnp.where(head_of_lane == h, normal[h * rows : (h + 1) * rows], result)
        attended[:, g * CHUNK : (g + 1) * CHUNK] = result

    def pass_z(g):
        @pl.when(z_gets)
        def _():
            relay(g, y_slot, z_slot, z_send, z_recv, z_to).wait_recv()

        @pl.when(jnp.logical_and(z_gets, jnp.logical_not(outer)))
        def _():
            c_copy(g, c_target).start()

    local[3].wait()
    for g in range(chunks):
        make_bias(g)
        for part in range(2):
            y_copy(g, part, y_slot).wait_recv()
        pl.when(z_sends)(lambda g=g: z_copy(g).start())
        pl.when(outer)(lambda g=g: c_copy(g, c_target).start())
        if g >= 1:
            pass_z(g - 1)
        if g >= 2:
            attend(g - 2)
    pass_z(chunks - 1)
    for g in range(max(0, chunks - 2), chunks):
        attend(g)

    for copy in local[4:7]:
        copy.wait()
    mid = (
        frames[...].astype(jnp.float32)
        + jnp.dot(attended[...], out_w[...], preferred_element_type=jnp.float32)
    ).astype(jnp.bfloat16)
    frames[...] = mid
    normed = layer_norm(mid.astype(jnp.float32), norm_gain[...]).astype(jnp.bfloat16)
    local[7].wait()

    def to_prev(j):
        cols = pl.ds(j * GATE_COLS, GATE_COLS)
        return remote(
            gated.at[pl.ds(HALO, HALO), cols],
            gated.at[pl.ds(HALO + rows, HALO), cols],
            h_send.at[0, j],
            h_recv.at[0, j],
            me - 1,
        )

    def to_next(j):
        cols = pl.ds(j * GATE_COLS, GATE_COLS)
        return remote(
            gated.at[pl.ds(rows, HALO), cols],
            gated.at[pl.ds(0, HALO), cols],
            h_send.at[1, j],
            h_recv.at[1, j],
            me + 1,
        )

    has_prev = me > 0
    has_next = me < seq_count - 1
    for j in range(gate_chunks):
        first = j * GATE_COLS
        cols = slice(first, first + GATE_COLS)
        linear = jnp.dot(normed, expand[:, cols], preferred_element_type=jnp.float32)
        gate = jnp.dot(
            normed,
            expand[:, width + first : width + first + GATE_COLS],
            preferred_element_type=jnp.float32,
        )
        units = (linear * jax.nn.sigmoid(gate)).astype(jnp.bfloat16)
        gated[HALO : HALO + rows, cols] = units
        pl.when(has_prev)(lambda j=j: to_prev(j).start())
        pl.when(has_next)(lambda j=j: to_next(j).start())
        wide = units.astype(jnp.float32)
        plain[HALO : HALO + rows, cols] = wide
        offset4[HALO - 4 : HALO - 4 + rows, cols] = wide

    local[8].wait()

    def first_row(i, t):
        return i * CONV_ROWS + HALO + DILATION * (t - KERNEL // 2)

    def is_own(i, t):
        return first_row(i, t) >= HALO and first_row(i, t) + CONV_ROWS <= HALO + rows

    def add_taps(total, i, cols, chosen):
        for t in chosen:
            row = first_row(i, t)
            source = plain if row % 8 == 0 else offset4
            row -= row % 8
            term = taps[t : t + 1, cols] * source[row : row + CONV_ROWS, cols]
            total = term if total is None else total + term
        return total

    tiles = [
        (i, slice(c * CONV_COLS, (c + 1) * CONV_COLS))
        for c in range(width // CONV_COLS)
        for i in range(rows // CONV_ROWS)
    ]
    for i, cols in tiles:
        conv[i * CONV_ROWS : (i + 1) * CONV_ROWS, cols] = add_taps(
            None, i, cols, [t for t in range(KERNEL) if is_own(i, t)]
        )

    for j in range(gate_chunks):
        pl.when(has_next)(lambda j=j: to_prev(j).wait_recv())
        pl.when(has_prev)(lambda j=j: to_next(j).wait_recv())
    left = gated[0:HALO, :].astype(jnp.float32)
    right = gated[HALO + rows : 2 * HALO + rows, :].astype(jnp.float32)
    plain[0:HALO, :] = left
    plain[HALO + rows : 2 * HALO + rows, :] = right
    offset4[0 : HALO - 4, :] = left[4:HALO]
    offset4[HALO - 4 + rows : 2 * HALO - 4 + rows, :] = right
    for i, cols in tiles:
        here = slice(i * CONV_ROWS, (i + 1) * CONV_ROWS)
        conv[here, cols] = add_taps(
            conv[here, cols], i, cols, [t for t in range(KERNEL) if not is_own(i, t)]
        )

    local[9].wait()
    inner = layer_norm(conv[...], inner_gain[...])
    activated = (inner * jax.nn.sigmoid(inner)).astype(jnp.bfloat16)
    local[10].wait()
    out[...] = (
        frames[...].astype(jnp.float32)
        + jnp.dot(activated, shrink[...], preferred_element_type=jnp.float32)
    ).astype(jnp.bfloat16)

    for g in range(chunks):
        for part in range(2):
            y_copy(g, part, y_target).wait_send()
            p_copy(g, part, p_target).wait_send()
        pl.when(z_sends)(lambda g=g: z_copy(g).wait_send())
        pl.when(c_sends)(lambda g=g: c_copy(g, c_target).wait_send())
    for j in range(gate_chunks):
        pl.when(has_prev)(lambda j=j: to_prev(j).wait_send())
        pl.when(has_next)(lambda j=j: to_next(j).wait_send())


def on_device(
    frames_in,
    query_proj,
    key_proj,
    value_proj,
    utterance_lengths,
    bucket_table,
    bucket_bias,
    out_weight,
    norm_gain,
    expand_weight,
    depth_taps,
    inner_gain,
    shrink_weight,
):
    rows, width = frames_in.shape
    att_width = query_proj.shape[1]
    chunks = att_width // CHUNK
    gate_chunks = width // GATE_COLS
    window = SLOTS * rows
    heads_here = CHUNK // (att_width // bucket_bias.shape[1])
    wide_rows = rows + 2 * HALO
    bf16, f32 = jnp.bfloat16, jnp.float32
    vmem = pl.BlockSpec(memory_space=pltpu.VMEM)
    anywhere = pl.BlockSpec(memory_space=pl.ANY)
    dma = pltpu.SemaphoreType.DMA
    return pl.pallas_call(
        functools.partial(kernel, lax.axis_size("seq")),
        out_shape=jax.ShapeDtypeStruct((rows, width), bf16),
        in_specs=[anywhere] * 13,
        out_specs=vmem,
        scratch_shapes=[
            pltpu.SMEM(utterance_lengths.shape, jnp.int32),
            pltpu.VMEM(bucket_table.shape, jnp.int32),
            pltpu.VMEM(bucket_bias.shape[::-1], f32),
            pltpu.VMEM((1, width), f32),
            pltpu.VMEM((1, width), f32),
            pltpu.VMEM((rows, width), bf16),
            pltpu.VMEM((rows, att_width), bf16),
            pltpu.VMEM(out_weight.shape, bf16),
            pltpu.VMEM(expand_weight.shape, bf16),
            pltpu.VMEM(depth_taps.shape, f32),
            pltpu.VMEM(shrink_weight.shape, bf16),
            pltpu.VMEM((chunks, 2, window, CHUNK), bf16),
            pltpu.VMEM((1, window + rows), jnp.int32),
            pltpu.VMEM((chunks, heads_here * rows, window), f32),
            pltpu.VMEM((rows, att_width), bf16),
            pltpu.VMEM((wide_rows, width), bf16),
            pltpu.VMEM((wide_rows, width), f32),
            pltpu.VMEM((wide_rows, width), f32),
            pltpu.VMEM((rows, width), f32),
            dma((11,)),
            dma((chunks, 2)),
            dma((chunks, 2)),
            dma((chunks, 2)),
            dma((chunks, 2)),
            dma((chunks, 2)),
            dma((chunks,)),
            dma((chunks,)),
            dma((chunks,)),
            dma((chunks,)),
            dma((2, gate_chunks)),
            dma((2, gate_chunks)),
        ],
        compiler_params=pltpu.CompilerParams(
            collective_id=0, has_side_effects=True, vmem_limit_bytes=60 * 1024 * 1024
        ),
    )(
        utterance_lengths,
        bucket_table,
        bucket_bias.T,
        norm_gain.reshape(1, -1),
        inner_gain.reshape(1, -1),
        frames_in,
        query_proj,
        key_proj,
        value_proj,
        out_weight,
        expand_weight,
        depth_taps,
        shrink_weight,
    )


def solution(mesh):
    placed = (
        P(("groups", "seq"), None),
        P(("groups", "seq"), None),
        P(("groups", "seq"), None),
        P(("groups", "seq"), None),
        P("groups"),
        P(),
        P(),
        P(),
        P(),
        P(),
        P(),
        P(),
        P(),
    )
    return jax.shard_map(
        on_device, mesh=mesh, in_specs=placed, out_specs=P(("groups", "seq"), None), check_vma=False
    )
```

```python
import functools

import jax
import jax.numpy as jnp
from jax import lax
from jax.experimental import pallas as pl
from jax.experimental.pallas import tpu as pltpu
from jax.sharding import PartitionSpec as P

KERNEL = 31
DILATION = 4
REACH = 2
SLOTS = 2 * REACH + 1
CHUNK = 128
GATE_COLS = 256
HALO = 64
CONV_ROWS = 32
CONV_COLS = 512

norm_epsilon = 1e-05
masked_score = -1e30


def layer_norm(values, gain_vec):
    row_mean = jnp.mean(values, axis=-1, keepdims=True)
    centred = values - row_mean
    spread = jnp.mean(centred * centred, axis=-1, keepdims=True)
    return centred * lax.rsqrt(spread + norm_epsilon) * gain_vec


def kernel(
    seq_count,
    lengths_hbm,
    table_hbm,
    bucket_bias_hbm,
    norm_gain_hbm,
    inner_gain_hbm,
    frames_hbm,
    query_hbm,
    key_hbm,
    value_hbm,
    out_w_hbm,
    expand_hbm,
    taps_hbm,
    shrink_hbm,
    out,
    lengths,
    table,
    bucket_bias,
    norm_gain,
    inner_gain,
    frames,
    query,
    out_w,
    expand,
    taps,
    shrink,
    kv,
    table_pad,
    bias,
    attended,
    gated,
    plain,
    offset4,
    conv,
    result,
    local_sem,
    own_sem,
    p_send,
    p_recv,
    y_send,
    y_recv,
    z_send,
    z_recv,
    c_send,
    c_recv,
    h_send,
    h_recv,
    out_sem,
):
    rows, width = frames.shape
    att_width = query.shape[1]
    chunks = att_width // CHUNK
    head_width = att_width // bucket_bias.shape[0]
    window = SLOTS * rows
    gate_chunks = width // GATE_COLS

    me = lax.axis_index("seq")
    core = lax.rem(me, 2)
    is_a = lax.rem(me, 4) < 2
    outer = is_a == (core == 0)
    partner = me + 1 - 2 * core
    y_peer = jnp.where(is_a, me + 2, me - 2)
    z_to = jnp.where(is_a, me + 4, me - 4)
    z_from = jnp.where(is_a, me - 4, me + 4)
    beside = jnp.where(core == 0, me - 1, me + 1)
    z_sends = jnp.logical_and(z_to >= 0, z_to < seq_count)
    z_gets = jnp.logical_and(z_from >= 0, z_from < seq_count)
    beside_is = jnp.logical_and(beside >= 0, beside < seq_count)
    c_sends = jnp.logical_or(outer, z_gets)
    c_gets = jnp.logical_or(jnp.logical_not(outer), z_gets)
    y_slot = jnp.where(is_a, 4, 0)
    z_slot = jnp.where(is_a, 0, 4)
    c_slot = jnp.where(core == 0, 1, 3)

    def slot_rows(slot):
        return pl.ds(pl.multiple_of(slot * rows, rows), rows)

    own = []
    for part, source in enumerate((key_hbm, value_hbm)):
        for g in range(chunks):
            own.append(
                pltpu.make_async_copy(
                    source.at[:, pl.ds(g * CHUNK, CHUNK)],
                    kv.at[g, part, pl.ds(REACH * rows, rows), :],
                    own_sem.at[g, part],
                )
            )
    local = [
        pltpu.make_async_copy(source, target, local_sem.at[i])
        for i, (source, target) in enumerate(
            (
                (lengths_hbm, lengths),
                (table_hbm, table),
                (bucket_bias_hbm, bucket_bias),
                (query_hbm, query),
                (frames_hbm, frames),
                (out_w_hbm, out_w),
                (norm_gain_hbm, norm_gain),
                (expand_hbm, expand),
                (taps_hbm, taps),
                (inner_gain_hbm, inner_gain),
                (shrink_hbm, shrink),
            )
        )
    ]

    barrier = pltpu.get_barrier_semaphore()

    def greet(device):
        pl.semaphore_signal(
            barrier, inc=1, device_id={"seq": device}, device_id_type=pl.DeviceIdType.MESH
        )

    greet(partner)
    greet(y_peer)
    pl.when(z_sends)(lambda: greet(z_to))
    pl.when(z_gets)(lambda: greet(z_from))
    pl.when(beside_is)(lambda: greet(beside))
    for copy in local[:4] + own:
        copy.start()
    greetings = (
        2 + z_sends.astype(jnp.int32) + z_gets.astype(jnp.int32) + beside_is.astype(jnp.int32)
    )
    pl.semaphore_wait(barrier, greetings)

    def remote(source, target, send, recv, device):
        return pltpu.make_async_remote_copy(
            src_ref=source,
            dst_ref=target,
            send_sem=send,
            recv_sem=recv,
            device_id={"seq": device},
            device_id_type=pl.DeviceIdType.MESH,
        )

    def own_copy(g, part, slot, send, recv, device):
        source = (key_hbm, value_hbm)[part]
        return remote(
            source.at[:, pl.ds(g * CHUNK, CHUNK)],
            kv.at[g, part, slot_rows(slot), :],
            send.at[g, part],
            recv.at[g, part],
            device,
        )

    def relay(g, part, from_slot, to_slot, send, recv, device):
        return remote(
            kv.at[g, part, slot_rows(from_slot), :],
            kv.at[g, part, slot_rows(to_slot), :],
            send.at[g, part],
            recv.at[g, part],
            device,
        )

    def y_copy(g, part, slot):
        return own_copy(g, part, slot, y_send, y_recv, y_peer)

    def p_copy(g, part, slot):
        return own_copy(g, part, slot, p_send, p_recv, partner)

    y_target = jnp.where(is_a, 0, 4)
    p_target = 2 * core + 1
    p_slot = 3 - 2 * core
    c_target = jnp.where(core == 0, 3, 1)
    c_source = jnp.where(outer, y_slot, z_slot)

    def z_copy(g, part):
        return relay(g, part, y_slot, z_slot, z_send, z_recv, z_to)

    def c_copy(g, part, target):
        return relay(g, part, c_source, target, c_send, c_recv, partner)

    for g in range(chunks):
        for part in range(2):
            y_copy(g, part, y_target).start()
        for part in range(2):
            p_copy(g, part, p_target).start()
    for copy in local[4:]:
        copy.start()

    @pl.when(jnp.logical_not(z_gets))
    def _():
        for g in range(chunks):
            kv[g, :, slot_rows(z_slot), :] = jnp.zeros((2, rows, CHUNK), kv.dtype)

    @pl.when(jnp.logical_not(c_gets))
    def _():
        for g in range(chunks):
            kv[g, :, slot_rows(c_slot), :] = jnp.zeros((2, rows, CHUNK), kv.dtype)

    zero_halo = jnp.zeros((HALO, width), gated.dtype)

    @pl.when(me == 0)
    def _():
        gated[0:HALO, :] = zero_halo

    @pl.when(me == seq_count - 1)
    def _():
        gated[HALO + rows : 2 * HALO + rows, :] = zero_halo

    for copy in local[:3]:
        copy.wait()

    query_at = me * rows + lax.broadcasted_iota(jnp.int32, (rows, 1), 0)
    key_at = (me - REACH) * rows + lax.broadcasted_iota(jnp.int32, (1, window), 1)

    def count(u, state):
        bound, query_seg, key_seg = state
        bound = bound + lengths[u]
        return (
            bound,
            query_seg + (query_at >= bound).astype(jnp.int32),
            key_seg + (key_at >= bound).astype(jnp.int32),
        )

    utterances = lengths.shape[0]
    _, query_seg, key_seg = lax.fori_loop(
        0,
        utterances,
        count,
        (jnp.int32(0), jnp.zeros((rows, 1), jnp.int32), jnp.zeros((1, window), jnp.int32)),
        unroll=utterances <= 32,
    )
    key_seg = jnp.where(key_at < 0, -1, key_seg)

    line_length = table.shape[0]
    padded_length = window + rows
    table_pad[...] = jnp.zeros_like(table_pad)
    table_pad[:, 0:line_length] = table[...].reshape(1, line_length)
    buckets = bucket_bias.shape[1]
    hits = (
        lax.broadcasted_iota(jnp.int32, (buckets, padded_length), 0) == table_pad[...]
    ).astype(jnp.float32)
    bias_line = jnp.dot(
        bucket_bias[...],
        hits,
        precision=lax.Precision.HIGHEST,
        preferred_element_type=jnp.float32,
    )
    heads_here = CHUNK // head_width

    def make_bias(g):
        same = query_seg == key_seg
        for h in range(heads_here):
            head = g * heads_here + h
            line = jnp.broadcast_to(bias_line[head : head + 1, :], (8, padded_length))
            skewed = pltpu.roll(line, padded_length - (rows - 1), 1, stride=1, stride_axis=0)
            for first in range(0, rows, 8):
                block = skewed if first == 0 else pltpu.roll(skewed, first, 1)
                bias[g, h * rows + first : h * rows + first + 8, :] = jnp.where(
                    same[first : first + 8], block[:, :window], masked_score
                )

    head_of_lane = lax.broadcasted_iota(jnp.int32, (rows, CHUNK), 1) // head_width

    def attend(g):
        for part in range(2):
            own[part * chunks + g].wait()
            p_copy(g, part, p_slot).wait_recv()

        @pl.when(c_gets)
        def _():
            for part in range(2):
                c_copy(g, part, c_slot).wait_recv()

        chunk_query = query[:, g * CHUNK : (g + 1) * CHUNK]
        stacked = jnp.concatenate(
            [
                jnp.where(head_of_lane == h, chunk_query, jnp.zeros_like(chunk_query))
                for h in range(heads_here)
            ],
            axis=0,
        )
        scores = lax.dot_general(
            stacked, kv[g, 0], (((1,), (1,)), ((), ())), preferred_element_type=jnp.float32
        )
        scores = scores * (head_width**-0.5) + bias[g]
        top = jnp.max(scores, axis=1, keepdims=True)
        weights = jnp.exp(scores - top)
        values_and_ones = jnp.concatenate([kv[g, 1], jnp.ones_like(kv[g, 1])], axis=1)
        weighted = jnp.dot(
            weights.astype(jnp.bfloat16), values_and_ones, preferred_element_type=jnp.float32
        )
        normal = (weighted[:, :CHUNK] / weighted[:, CHUNK:]).astype(jnp.bfloat16)
        chosen = normal[0:rows]
        for h in range(1, heads_here):
            chosen = jnp.where(head_of_lane == h, normal[h * rows : (h + 1) * rows], chosen)
        attended[:, g * CHUNK : (g + 1) * CHUNK] = chosen

    def pass_y(g):
        for part in range(2):
            y_copy(g, part, y_slot).wait_recv()
            pl.when(z_sends)(z_copy(g, part).start)
            pl.when(outer)(c_copy(g, part, c_target).start)

    def pass_z(g):
        for part in range(2):

            @pl.when(z_gets)
            def _():
                relay(g, part, y_slot, z_slot, z_send, z_recv, z_to).wait_recv()

            @pl.when(jnp.logical_and(z_gets, jnp.logical_not(outer)))
            def _():
                c_copy(g, part, c_target).start()

    local[3].wait()
    make_bias(0)
    for g in range(chunks):
        if g + 1 < chunks:
            make_bias(g + 1)
        pass_y(g)
        if g >= 1:
            pass_z(g - 1)
        if g >= 2:
            attend(g - 2)
    pass_z(chunks - 1)
    for g in range(max(0, chunks - 2), chunks):
        attend(g)

    for copy in local[4:7]:
        copy.wait()
    mid = (
        frames[...].astype(jnp.float32)
        + jnp.dot(attended[...], out_w[...], preferred_element_type=jnp.float32)
    ).astype(jnp.bfloat16)
    frames[...] = mid
    normed = layer_norm(mid.astype(jnp.float32), norm_gain[...]).astype(jnp.bfloat16)
    local[7].wait()

    def to_prev(j):
        cols = pl.ds(j * GATE_COLS, GATE_COLS)
        return remote(
            gated.at[pl.ds(HALO, HALO), cols],
            gated.at[pl.ds(HALO + rows, HALO), cols],
            h_send.at[0, j],
            h_recv.at[0, j],
            me - 1,
        )

    def to_next(j):
        cols = pl.ds(j * GATE_COLS, GATE_COLS)
        return remote(
            gated.at[pl.ds(rows, HALO), cols],
            gated.at[pl.ds(0, HALO), cols],
            h_send.at[1, j],
            h_recv.at[1, j],
            me + 1,
        )

    has_prev = me > 0
    has_next = me < seq_count - 1
    for j in range(gate_chunks):
        first = j * GATE_COLS
        cols = slice(first, first + GATE_COLS)
        linear = jnp.dot(normed, expand[:, cols], preferred_element_type=jnp.float32)
        gate = jnp.dot(
            normed,
            expand[:, width + first : width + first + GATE_COLS],
            preferred_element_type=jnp.float32,
        )
        units = (linear * jax.nn.sigmoid(gate)).astype(jnp.bfloat16)
        gated[HALO : HALO + rows, cols] = units
        pl.when(has_prev)(lambda j=j: to_prev(j).start())
        pl.when(has_next)(lambda j=j: to_next(j).start())
        wide = units.astype(jnp.float32)
        plain[HALO : HALO + rows, cols] = wide
        offset4[HALO - 4 : HALO - 4 + rows, cols] = wide

    local[8].wait()

    def first_row(i, t):
        return i * CONV_ROWS + HALO + DILATION * (t - KERNEL // 2)

    def is_own(i, t):
        return first_row(i, t) >= HALO and first_row(i, t) + CONV_ROWS <= HALO + rows

    def add_taps(total, i, cols, chosen):
        for t in chosen:
            row = first_row(i, t)
            source = plain if row % 8 == 0 else offset4
            row -= row % 8
            term = taps[t : t + 1, cols] * source[row : row + CONV_ROWS, cols]
            total = term if total is None else total + term
        return total

    tiles = [
        (i, slice(c * CONV_COLS, (c + 1) * CONV_COLS))
        for c in range(width // CONV_COLS)
        for i in range(rows // CONV_ROWS)
    ]
    for i, cols in tiles:
        conv[i * CONV_ROWS : (i + 1) * CONV_ROWS, cols] = add_taps(
            None, i, cols, [t for t in range(KERNEL) if is_own(i, t)]
        )

    for c in range(width // CONV_COLS):
        half = slice(c * CONV_COLS, (c + 1) * CONV_COLS)
        for j in range(half.start // GATE_COLS, half.stop // GATE_COLS):
            pl.when(has_next)(lambda j=j: to_prev(j).wait_recv())
            pl.when(has_prev)(lambda j=j: to_next(j).wait_recv())
        left = gated[0:HALO, half].astype(jnp.float32)
        right = gated[HALO + rows : 2 * HALO + rows, half].astype(jnp.float32)
        plain[0:HALO, half] = left
        plain[HALO + rows : 2 * HALO + rows, half] = right
        offset4[0 : HALO - 4, half] = left[4:HALO]
        offset4[HALO - 4 + rows : 2 * HALO - 4 + rows, half] = right
        for i in range(rows // CONV_ROWS):
            here = slice(i * CONV_ROWS, (i + 1) * CONV_ROWS)
            conv[here, half] = add_taps(
                conv[here, half], i, half, [t for t in range(KERNEL) if not is_own(i, t)]
            )

    local[9].wait()
    inner = layer_norm(conv[...], inner_gain[...])
    activated = (inner * jax.nn.sigmoid(inner)).astype(jnp.bfloat16)
    local[10].wait()
    leaving = []
    for j in range(gate_chunks):
        cols = slice(j * GATE_COLS, (j + 1) * GATE_COLS)
        result[:, cols] = (
            frames[:, cols].astype(jnp.float32)
            + jnp.dot(activated, shrink[:, cols], preferred_element_type=jnp.float32)
        ).astype(jnp.bfloat16)
        leaving.append(
            pltpu.make_async_copy(result.at[:, cols], out.at[:, cols], out_sem.at[j])
        )
        leaving[j].start()

    for g in range(chunks):
        for part in range(2):
            y_copy(g, part, y_target).wait_send()
            p_copy(g, part, p_target).wait_send()
            pl.when(z_sends)(z_copy(g, part).wait_send)
            pl.when(c_sends)(c_copy(g, part, c_target).wait_send)
    for j in range(gate_chunks):
        pl.when(has_prev)(lambda j=j: to_prev(j).wait_send())
        pl.when(has_next)(lambda j=j: to_next(j).wait_send())
    for copy in leaving:
        copy.wait()


def hand_over(source, target, sems):
    part_rows = source.shape[0] // sems.shape[0]
    copies = [
        pltpu.make_async_copy(
            source.at[pl.ds(i * part_rows, part_rows), :],
            target.at[pl.ds(i * part_rows, part_rows), :],
            sems.at[i],
        )
        for i in range(sems.shape[0])
    ]
    for copy in copies:
        copy.start()
    for copy in copies:
        copy.wait()


def on_device(
    frames_in,
    query_proj,
    key_proj,
    value_proj,
    utterance_lengths,
    bucket_table,
    bucket_bias,
    out_weight,
    norm_gain,
    expand_weight,
    depth_taps,
    inner_gain,
    shrink_weight,
):
    rows, width = frames_in.shape
    att_width = query_proj.shape[1]
    chunks = att_width // CHUNK
    gate_chunks = width // GATE_COLS
    window = SLOTS * rows
    heads_here = CHUNK // (att_width // bucket_bias.shape[1])
    wide_rows = rows + 2 * HALO
    bf16, f32 = jnp.bfloat16, jnp.float32
    anywhere = pl.BlockSpec(memory_space=pl.ANY)
    dma = pltpu.SemaphoreType.DMA
    block_out = pl.pallas_call(
        functools.partial(kernel, lax.axis_size("seq")),
        out_shape=jax.ShapeDtypeStruct((rows, width), bf16),
        in_specs=[anywhere] * 13,
        out_specs=anywhere,
        scratch_shapes=[
            pltpu.SMEM(utterance_lengths.shape, jnp.int32),
            pltpu.VMEM(bucket_table.shape, jnp.int32),
            pltpu.VMEM(bucket_bias.shape[::-1], f32),
            pltpu.VMEM((1, width), f32),
            pltpu.VMEM((1, width), f32),
            pltpu.VMEM((rows, width), bf16),
            pltpu.VMEM((rows, att_width), bf16),
            pltpu.VMEM(out_weight.shape, bf16),
            pltpu.VMEM(expand_weight.shape, bf16),
            pltpu.VMEM(depth_taps.shape, f32),
            pltpu.VMEM(shrink_weight.shape, bf16),
            pltpu.VMEM((chunks, 2, window, CHUNK), bf16),
            pltpu.VMEM((1, window + rows), jnp.int32),
            pltpu.VMEM((chunks, heads_here * rows, window), f32),
            pltpu.VMEM((rows, att_width), bf16),
            pltpu.VMEM((wide_rows, width), bf16),
            pltpu.VMEM((wide_rows, width), f32),
            pltpu.VMEM((wide_rows, width), f32),
            pltpu.VMEM((rows, width), f32),
            pltpu.VMEM((rows, width), bf16),
            dma((11,)),
            dma((chunks, 2)),
            dma((chunks, 2)),
            dma((chunks, 2)),
            dma((chunks, 2)),
            dma((chunks, 2)),
            dma((chunks, 2)),
            dma((chunks, 2)),
            dma((chunks, 2)),
            dma((chunks, 2)),
            dma((2, gate_chunks)),
            dma((2, gate_chunks)),
            dma((gate_chunks,)),
        ],
        compiler_params=pltpu.CompilerParams(
            collective_id=0, has_side_effects=True, vmem_limit_bytes=60 * 1024 * 1024
        ),
    )(
        utterance_lengths,
        bucket_table,
        bucket_bias.T,
        norm_gain.reshape(1, -1),
        inner_gain.reshape(1, -1),
        frames_in,
        query_proj,
        key_proj,
        value_proj,
        out_weight,
        expand_weight,
        depth_taps,
        shrink_weight,
    )
    return pl.pallas_call(
        hand_over,
        out_shape=jax.ShapeDtypeStruct((rows, width), bf16),
        in_specs=[anywhere],
        out_specs=anywhere,
        scratch_shapes=[dma((4,))],
        compiler_params=pltpu.CompilerParams(vmem_limit_bytes=60 * 1024 * 1024),
    )(block_out)


def solution(mesh):
    placed = (
        P(("groups", "seq"), None),
        P(("groups", "seq"), None),
        P(("groups", "seq"), None),
        P(("groups", "seq"), None),
        P("groups"),
        P(),
        P(),
        P(),
        P(),
        P(),
        P(),
        P(),
        P(),
    )
    return jax.shard_map(
        on_device, mesh=mesh, in_specs=placed, out_specs=P(("groups", "seq"), None), check_vma=False
    )
```

```python
import functools

import jax
import jax.numpy as jnp
from jax import lax
from jax.experimental import pallas as pl
from jax.experimental.pallas import tpu as pltpu
from jax.sharding import PartitionSpec as P

KERNEL = 31
DILATION = 4
REACH = 2
SLOTS = 2 * REACH + 1
CHUNK = 128
GATE_COLS = 256
HALO = 64
CONV_ROWS = 32
CONV_COLS = 512

norm_epsilon = 1e-05
masked_score = -1e30


def layer_norm(values, gain_vec):
    row_mean = jnp.mean(values, axis=-1, keepdims=True)
    centred = values - row_mean
    spread = jnp.mean(centred * centred, axis=-1, keepdims=True)
    return centred * lax.rsqrt(spread + norm_epsilon) * gain_vec


def kernel(
    seq_count,
    lengths_hbm,
    table_hbm,
    bucket_bias_hbm,
    norm_gain_hbm,
    inner_gain_hbm,
    frames_hbm,
    query_hbm,
    key_hbm,
    value_hbm,
    out_w_hbm,
    expand_hbm,
    taps_hbm,
    shrink_hbm,
    out,
    lengths,
    table,
    bucket_bias,
    norm_gain,
    inner_gain,
    frames,
    query,
    out_w,
    expand,
    taps,
    shrink,
    kv,
    table_pad,
    bias,
    attended,
    gated,
    plain,
    offset4,
    conv,
    result,
    weights,
    local_sem,
    own_sem,
    p_send,
    p_recv,
    y_send,
    y_recv,
    z_send,
    z_recv,
    c_send,
    c_recv,
    h_send,
    h_recv,
    out_sem,
):
    rows, width = frames.shape
    att_width = query.shape[1]
    chunks = att_width // CHUNK
    head_width = att_width // bucket_bias.shape[0]
    window = SLOTS * rows
    gate_chunks = width // GATE_COLS

    me = lax.axis_index("seq")
    core = lax.rem(me, 2)
    is_a = lax.rem(me, 4) < 2
    outer = is_a == (core == 0)
    partner = me + 1 - 2 * core
    y_peer = jnp.where(is_a, me + 2, me - 2)
    z_to = jnp.where(is_a, me + 4, me - 4)
    z_from = jnp.where(is_a, me - 4, me + 4)
    beside = jnp.where(core == 0, me - 1, me + 1)
    z_sends = jnp.logical_and(z_to >= 0, z_to < seq_count)
    z_gets = jnp.logical_and(z_from >= 0, z_from < seq_count)
    beside_is = jnp.logical_and(beside >= 0, beside < seq_count)
    c_sends = jnp.logical_or(outer, z_gets)
    c_gets = jnp.logical_or(jnp.logical_not(outer), z_gets)
    y_slot = jnp.where(is_a, 4, 0)
    z_slot = jnp.where(is_a, 0, 4)
    c_slot = jnp.where(core == 0, 1, 3)

    def slot_rows(slot):
        return pl.ds(pl.multiple_of(slot * rows, rows), rows)

    own = []
    for part, source in enumerate((key_hbm, value_hbm)):
        for g in range(chunks):
            own.append(
                pltpu.make_async_copy(
                    source.at[:, pl.ds(g * CHUNK, CHUNK)],
                    kv.at[g, part, pl.ds(REACH * rows, rows), :],
                    own_sem.at[g, part],
                )
            )
    local = [
        pltpu.make_async_copy(source, target, local_sem.at[i])
        for i, (source, target) in enumerate(
            (
                (lengths_hbm, lengths),
                (table_hbm, table),
                (bucket_bias_hbm, bucket_bias),
                (query_hbm, query),
                (frames_hbm, frames),
                (out_w_hbm, out_w),
                (norm_gain_hbm, norm_gain),
                (expand_hbm, expand),
                (taps_hbm, taps),
                (inner_gain_hbm, inner_gain),
                (shrink_hbm, shrink),
            )
        )
    ]

    barrier = pltpu.get_barrier_semaphore()

    def greet(device):
        pl.semaphore_signal(
            barrier, inc=1, device_id={"seq": device}, device_id_type=pl.DeviceIdType.MESH
        )

    greet(partner)
    greet(y_peer)
    pl.when(z_sends)(lambda: greet(z_to))
    pl.when(z_gets)(lambda: greet(z_from))
    pl.when(beside_is)(lambda: greet(beside))
    for copy in local[:4] + own:
        copy.start()
    greetings = (
        2 + z_sends.astype(jnp.int32) + z_gets.astype(jnp.int32) + beside_is.astype(jnp.int32)
    )
    pl.semaphore_wait(barrier, greetings)

    def remote(source, target, send, recv, device):
        return pltpu.make_async_remote_copy(
            src_ref=source,
            dst_ref=target,
            send_sem=send,
            recv_sem=recv,
            device_id={"seq": device},
            device_id_type=pl.DeviceIdType.MESH,
        )

    def own_copy(g, part, slot, send, recv, device):
        source = (key_hbm, value_hbm)[part]
        return remote(
            source.at[:, pl.ds(g * CHUNK, CHUNK)],
            kv.at[g, part, slot_rows(slot), :],
            send.at[g, part],
            recv.at[g, part],
            device,
        )

    def relay(g, part, from_slot, to_slot, send, recv, device):
        return remote(
            kv.at[g, part, slot_rows(from_slot), :],
            kv.at[g, part, slot_rows(to_slot), :],
            send.at[g, part],
            recv.at[g, part],
            device,
        )

    def y_copy(g, part, slot):
        return own_copy(g, part, slot, y_send, y_recv, y_peer)

    def p_copy(g, part, slot):
        return own_copy(g, part, slot, p_send, p_recv, partner)

    y_target = jnp.where(is_a, 0, 4)
    p_target = 2 * core + 1
    p_slot = 3 - 2 * core
    c_target = jnp.where(core == 0, 3, 1)
    c_source = jnp.where(outer, y_slot, z_slot)

    def z_copy(g, part):
        return relay(g, part, y_slot, z_slot, z_send, z_recv, z_to)

    def c_copy(g, part, target):
        return relay(g, part, c_source, target, c_send, c_recv, partner)

    pieces = [(g, part) for part in range(2) for g in range(chunks)]
    for g, part in pieces:
        y_copy(g, part, y_target).start()
        p_copy(g, part, p_target).start()
    for copy in local[4:]:
        copy.start()

    @pl.when(jnp.logical_not(z_gets))
    def _():
        for g in range(chunks):
            kv[g, :, slot_rows(z_slot), :] = jnp.zeros((2, rows, CHUNK), kv.dtype)

    @pl.when(jnp.logical_not(c_gets))
    def _():
        for g in range(chunks):
            kv[g, :, slot_rows(c_slot), :] = jnp.zeros((2, rows, CHUNK), kv.dtype)

    zero_halo = jnp.zeros((HALO, width), gated.dtype)

    @pl.when(me == 0)
    def _():
        gated[0:HALO, :] = zero_halo

    @pl.when(me == seq_count - 1)
    def _():
        gated[HALO + rows : 2 * HALO + rows, :] = zero_halo

    for copy in local[:3]:
        copy.wait()

    query_at = me * rows + lax.broadcasted_iota(jnp.int32, (rows, 1), 0)
    key_at = (me - REACH) * rows + lax.broadcasted_iota(jnp.int32, (1, window), 1)

    def count(u, state):
        bound, query_seg, key_seg = state
        bound = bound + lengths[u]
        return (
            bound,
            query_seg + (query_at >= bound).astype(jnp.int32),
            key_seg + (key_at >= bound).astype(jnp.int32),
        )

    utterances = lengths.shape[0]
    _, query_seg, key_seg = lax.fori_loop(
        0,
        utterances,
        count,
        (jnp.int32(0), jnp.zeros((rows, 1), jnp.int32), jnp.zeros((1, window), jnp.int32)),
        unroll=utterances <= 32,
    )
    key_seg = jnp.where(key_at < 0, -1, key_seg)

    line_length = table.shape[0]
    padded_length = window + rows
    table_pad[...] = jnp.zeros_like(table_pad)
    table_pad[:, 0:line_length] = table[...].reshape(1, line_length)
    buckets = bucket_bias.shape[1]
    hits = (
        lax.broadcasted_iota(jnp.int32, (buckets, padded_length), 0) == table_pad[...]
    ).astype(jnp.float32)
    bias_line = jnp.dot(
        bucket_bias[...],
        hits,
        precision=lax.Precision.HIGHEST,
        preferred_element_type=jnp.float32,
    )
    heads_here = CHUNK // head_width

    def make_bias(g):
        same = query_seg == key_seg
        for h in range(heads_here):
            head = g * heads_here + h
            line = jnp.broadcast_to(bias_line[head : head + 1, :], (8, padded_length))
            skewed = pltpu.roll(line, padded_length - (rows - 1), 1, stride=1, stride_axis=0)
            for first in range(0, rows, 8):
                block = skewed if first == 0 else pltpu.roll(skewed, first, 1)
                bias[g, h * rows + first : h * rows + first + 8, :] = jnp.where(
                    same[first : first + 8], block[:, :window], masked_score
                )

    head_of_lane = lax.broadcasted_iota(jnp.int32, (rows, CHUNK), 1) // head_width

    def arrive(g, part):
        own[part * chunks + g].wait()
        p_copy(g, part, p_slot).wait_recv()
        pl.when(c_gets)(c_copy(g, part, c_slot).wait_recv)

    def weigh(g):
        chunk_query = query[:, g * CHUNK : (g + 1) * CHUNK]
        stacked = jnp.concatenate(
            [
                jnp.where(head_of_lane == h, chunk_query, jnp.zeros_like(chunk_query))
                for h in range(heads_here)
            ],
            axis=0,
        )
        scores = lax.dot_general(
            stacked, kv[g, 0], (((1,), (1,)), ((), ())), preferred_element_type=jnp.float32
        )
        scores = scores * (head_width**-0.5) + bias[g]
        top = jnp.max(scores, axis=1, keepdims=True)
        weights[g] = jnp.exp(scores - top).astype(jnp.bfloat16)

    def attend(g):
        values_and_ones = jnp.concatenate([kv[g, 1], jnp.ones_like(kv[g, 1])], axis=1)
        weighted = jnp.dot(weights[g], values_and_ones, preferred_element_type=jnp.float32)
        normal = (weighted[:, :CHUNK] / weighted[:, CHUNK:]).astype(jnp.bfloat16)
        chosen = normal[0:rows]
        for h in range(1, heads_here):
            chosen = jnp.where(head_of_lane == h, normal[h * rows : (h + 1) * rows], chosen)
        attended[:, g * CHUNK : (g + 1) * CHUNK] = chosen

    def use(g, part):
        arrive(g, part)
        (weigh, attend)[part](g)

    def pass_y(g, part):
        y_copy(g, part, y_slot).wait_recv()
        pl.when(z_sends)(z_copy(g, part).start)
        pl.when(outer)(c_copy(g, part, c_target).start)

    def pass_z(g, part):
        @pl.when(z_gets)
        def _():
            relay(g, part, y_slot, z_slot, z_send, z_recv, z_to).wait_recv()

        @pl.when(jnp.logical_and(z_gets, jnp.logical_not(outer)))
        def _():
            c_copy(g, part, c_target).start()

    half_att = att_width // 2

    def project(half):
        part = slice(half * half_att, (half + 1) * half_att)
        return jnp.dot(attended[:, part], out_w[part, :], preferred_element_type=jnp.float32)

    local[3].wait()
    make_bias(0)
    make_bias(1)
    for step, (g, part) in enumerate(pieces):
        pass_y(g, part)
        if step >= 1:
            pass_z(*pieces[step - 1])
        if part == 0 and g + 2 < chunks:
            make_bias(g + 2)
        if step >= 2:
            use(*pieces[step - 2])
    use(*pieces[-2])
    for copy in local[4:7]:
        copy.wait()
    conv[...] = frames[...].astype(jnp.float32) + project(0)
    pass_z(*pieces[-1])
    use(*pieces[-1])

    mid = (conv[...] + project(1)).astype(jnp.bfloat16)
    frames[...] = mid
    normed = layer_norm(mid.astype(jnp.float32), norm_gain[...]).astype(jnp.bfloat16)
    local[7].wait()

    def to_prev(j):
        cols = pl.ds(j * GATE_COLS, GATE_COLS)
        return remote(
            gated.at[pl.ds(HALO, HALO), cols],
            gated.at[pl.ds(HALO + rows, HALO), cols],
            h_send.at[0, j],
            h_recv.at[0, j],
            me - 1,
        )

    def to_next(j):
        cols = pl.ds(j * GATE_COLS, GATE_COLS)
        return remote(
            gated.at[pl.ds(rows, HALO), cols],
            gated.at[pl.ds(0, HALO), cols],
            h_send.at[1, j],
            h_recv.at[1, j],
            me + 1,
        )

    has_prev = me > 0
    has_next = me < seq_count - 1
    for j in range(gate_chunks):
        first = j * GATE_COLS
        cols = slice(first, first + GATE_COLS)
        linear = jnp.dot(normed, expand[:, cols], preferred_element_type=jnp.float32)
        gate = jnp.dot(
            normed,
            expand[:, width + first : width + first + GATE_COLS],
            preferred_element_type=jnp.float32,
        )
        units = (linear * jax.nn.sigmoid(gate)).astype(jnp.bfloat16)
        gated[HALO : HALO + rows, cols] = units
        pl.when(has_prev)(lambda j=j: to_prev(j).start())
        pl.when(has_next)(lambda j=j: to_next(j).start())
        wide = units.astype(jnp.float32)
        plain[HALO : HALO + rows, cols] = wide
        offset4[HALO - 4 : HALO - 4 + rows, cols] = wide

    local[8].wait()

    def first_row(i, t):
        return i * CONV_ROWS + HALO + DILATION * (t - KERNEL // 2)

    def is_own(i, t):
        return first_row(i, t) >= HALO and first_row(i, t) + CONV_ROWS <= HALO + rows

    def add_taps(total, i, cols, chosen):
        for t in chosen:
            row = first_row(i, t)
            source = plain if row % 8 == 0 else offset4
            row -= row % 8
            term = taps[t : t + 1, cols] * source[row : row + CONV_ROWS, cols]
            total = term if total is None else total + term
        return total

    tiles = [
        (i, slice(c * CONV_COLS, (c + 1) * CONV_COLS))
        for c in range(width // CONV_COLS)
        for i in range(rows // CONV_ROWS)
    ]
    for i, cols in tiles:
        conv[i * CONV_ROWS : (i + 1) * CONV_ROWS, cols] = add_taps(
            None, i, cols, [t for t in range(KERNEL) if is_own(i, t)]
        )

    for c in range(width // CONV_COLS):
        half = slice(c * CONV_COLS, (c + 1) * CONV_COLS)
        for j in range(half.start // GATE_COLS, half.stop // GATE_COLS):
            pl.when(has_next)(lambda j=j: to_prev(j).wait_recv())
            pl.when(has_prev)(lambda j=j: to_next(j).wait_recv())
        left = gated[0:HALO, half].astype(jnp.float32)
        right = gated[HALO + rows : 2 * HALO + rows, half].astype(jnp.float32)
        plain[0:HALO, half] = left
        plain[HALO + rows : 2 * HALO + rows, half] = right
        offset4[0 : HALO - 4, half] = left[4:HALO]
        offset4[HALO - 4 + rows : 2 * HALO - 4 + rows, half] = right
        for i in range(rows // CONV_ROWS):
            here = slice(i * CONV_ROWS, (i + 1) * CONV_ROWS)
            conv[here, half] = add_taps(
                conv[here, half], i, half, [t for t in range(KERNEL) if not is_own(i, t)]
            )

    local[9].wait()
    inner = layer_norm(conv[...], inner_gain[...])
    activated = (inner * jax.nn.sigmoid(inner)).astype(jnp.bfloat16)
    local[10].wait()
    leaving = []
    for j in range(gate_chunks):
        cols = slice(j * GATE_COLS, (j + 1) * GATE_COLS)
        result[:, cols] = (
            frames[:, cols].astype(jnp.float32)
            + jnp.dot(activated, shrink[:, cols], preferred_element_type=jnp.float32)
        ).astype(jnp.bfloat16)
        leaving.append(
            pltpu.make_async_copy(result.at[:, cols], out.at[:, cols], out_sem.at[j])
        )
        leaving[j].start()

    for g in range(chunks):
        for part in range(2):
            y_copy(g, part, y_target).wait_send()
            p_copy(g, part, p_target).wait_send()
            pl.when(z_sends)(z_copy(g, part).wait_send)
            pl.when(c_sends)(c_copy(g, part, c_target).wait_send)
    for j in range(gate_chunks):
        pl.when(has_prev)(lambda j=j: to_prev(j).wait_send())
        pl.when(has_next)(lambda j=j: to_next(j).wait_send())
    for copy in leaving:
        copy.wait()


def hand_over(source, target, held, in_sems, out_sems):
    count = in_sems.shape[0]
    part_rows = source.shape[0] // count
    parts = [pl.ds(i * part_rows, part_rows) for i in range(count)]
    inward = [
        pltpu.make_async_copy(source.at[part, :], held.at[part, :], in_sems.at[i])
        for i, part in enumerate(parts)
    ]
    outward = [
        pltpu.make_async_copy(held.at[part, :], target.at[part, :], out_sems.at[i])
        for i, part in enumerate(parts)
    ]
    for copy in inward:
        copy.start()
    for first, second in zip(inward, outward):
        first.wait()
        second.start()
    for copy in outward:
        copy.wait()


def on_device(
    frames_in,
    query_proj,
    key_proj,
    value_proj,
    utterance_lengths,
    bucket_table,
    bucket_bias,
    out_weight,
    norm_gain,
    expand_weight,
    depth_taps,
    inner_gain,
    shrink_weight,
):
    rows, width = frames_in.shape
    att_width = query_proj.shape[1]
    chunks = att_width // CHUNK
    gate_chunks = width // GATE_COLS
    window = SLOTS * rows
    heads_here = CHUNK // (att_width // bucket_bias.shape[1])
    wide_rows = rows + 2 * HALO
    bf16, f32 = jnp.bfloat16, jnp.float32
    anywhere = pl.BlockSpec(memory_space=pl.ANY)
    dma = pltpu.SemaphoreType.DMA
    block_out = pl.pallas_call(
        functools.partial(kernel, lax.axis_size("seq")),
        out_shape=jax.ShapeDtypeStruct((rows, width), bf16),
        in_specs=[anywhere] * 13,
        out_specs=anywhere,
        scratch_shapes=[
            pltpu.SMEM(utterance_lengths.shape, jnp.int32),
            pltpu.VMEM(bucket_table.shape, jnp.int32),
            pltpu.VMEM(bucket_bias.shape[::-1], f32),
            pltpu.VMEM((1, width), f32),
            pltpu.VMEM((1, width), f32),
            pltpu.VMEM((rows, width), bf16),
            pltpu.VMEM((rows, att_width), bf16),
            pltpu.VMEM(out_weight.shape, bf16),
            pltpu.VMEM(expand_weight.shape, bf16),
            pltpu.VMEM(depth_taps.shape, f32),
            pltpu.VMEM(shrink_weight.shape, bf16),
            pltpu.VMEM((chunks, 2, window, CHUNK), bf16),
            pltpu.VMEM((1, window + rows), jnp.int32),
            pltpu.VMEM((chunks, heads_here * rows, window), f32),
            pltpu.VMEM((rows, att_width), bf16),
            pltpu.VMEM((wide_rows, width), bf16),
            pltpu.VMEM((wide_rows, width), f32),
            pltpu.VMEM((wide_rows, width), f32),
            pltpu.VMEM((rows, width), f32),
            pltpu.VMEM((rows, width), bf16),
            pltpu.VMEM((chunks, heads_here * rows, window), bf16),
            dma((11,)),
            dma((chunks, 2)),
            dma((chunks, 2)),
            dma((chunks, 2)),
            dma((chunks, 2)),
            dma((chunks, 2)),
            dma((chunks, 2)),
            dma((chunks, 2)),
            dma((chunks, 2)),
            dma((chunks, 2)),
            dma((2, gate_chunks)),
            dma((2, gate_chunks)),
            dma((gate_chunks,)),
        ],
        compiler_params=pltpu.CompilerParams(
            collective_id=0, has_side_effects=True, vmem_limit_bytes=60 * 1024 * 1024
        ),
    )(
        utterance_lengths,
        bucket_table,
        bucket_bias.T,
        norm_gain.reshape(1, -1),
        inner_gain.reshape(1, -1),
        frames_in,
        query_proj,
        key_proj,
        value_proj,
        out_weight,
        expand_weight,
        depth_taps,
        shrink_weight,
    )
    return pl.pallas_call(
        hand_over,
        out_shape=jax.ShapeDtypeStruct((rows, width), bf16),
        in_specs=[anywhere],
        out_specs=anywhere,
        scratch_shapes=[pltpu.VMEM((rows, width), bf16), dma((4,)), dma((4,))],
        compiler_params=pltpu.CompilerParams(vmem_limit_bytes=60 * 1024 * 1024),
    )(block_out)


def solution(mesh):
    placed = (
        P(("groups", "seq"), None),
        P(("groups", "seq"), None),
        P(("groups", "seq"), None),
        P(("groups", "seq"), None),
        P("groups"),
        P(),
        P(),
        P(),
        P(),
        P(),
        P(),
        P(),
        P(),
    )
    return jax.shard_map(
        on_device, mesh=mesh, in_specs=placed, out_specs=P(("groups", "seq"), None), check_vma=False
    )
```

```python
import functools

import jax
import jax.numpy as jnp
from jax import lax
from jax.experimental import pallas as pl
from jax.experimental.pallas import tpu as pltpu
from jax.sharding import PartitionSpec as P

KERNEL = 31
DILATION = 4
REACH = 2
SLOTS = 2 * REACH + 1
CHUNK = 128
GATE_COLS = 256
HALO = 64
IN_FLIGHT = 3
CONV_ROWS = 32
CONV_COLS = 512

norm_epsilon = 1e-05
masked_score = -1e30


def layer_norm(values, gain_vec):
    row_mean = jnp.mean(values, axis=-1, keepdims=True)
    centred = values - row_mean
    spread = jnp.mean(centred * centred, axis=-1, keepdims=True)
    return centred * lax.rsqrt(spread + norm_epsilon) * gain_vec


def kernel(
    seq_count,
    lengths_hbm,
    table_hbm,
    bucket_bias_hbm,
    norm_gain_hbm,
    inner_gain_hbm,
    frames_hbm,
    query_hbm,
    key_hbm,
    value_hbm,
    out_w_hbm,
    expand_hbm,
    taps_hbm,
    shrink_hbm,
    out,
    lengths,
    table,
    bucket_bias,
    norm_gain,
    inner_gain,
    frames,
    query,
    out_w,
    expand,
    taps,
    shrink,
    kv,
    table_pad,
    bias,
    attended,
    gated,
    plain,
    offset4,
    conv,
    result,
    weights,
    local_sem,
    own_sem,
    p_send,
    p_recv,
    y_send,
    y_recv,
    z_send,
    z_recv,
    c_send,
    c_recv,
    h_send,
    h_recv,
    out_sem,
):
    rows, width = frames.shape
    att_width = query.shape[1]
    chunks = att_width // CHUNK
    head_width = att_width // bucket_bias.shape[0]
    window = SLOTS * rows
    gate_chunks = width // GATE_COLS

    me = lax.axis_index("seq")
    core = lax.rem(me, 2)
    is_a = lax.rem(me, 4) < 2
    outer = is_a == (core == 0)
    partner = me + 1 - 2 * core
    y_peer = jnp.where(is_a, me + 2, me - 2)
    z_to = jnp.where(is_a, me + 4, me - 4)
    z_from = jnp.where(is_a, me - 4, me + 4)
    beside = jnp.where(core == 0, me - 1, me + 1)
    z_sends = jnp.logical_and(z_to >= 0, z_to < seq_count)
    z_gets = jnp.logical_and(z_from >= 0, z_from < seq_count)
    beside_is = jnp.logical_and(beside >= 0, beside < seq_count)
    c_sends = jnp.logical_or(outer, z_gets)
    c_gets = jnp.logical_or(jnp.logical_not(outer), z_gets)
    y_slot = jnp.where(is_a, 4, 0)
    z_slot = jnp.where(is_a, 0, 4)
    c_slot = jnp.where(core == 0, 1, 3)

    def slot_rows(slot):
        return pl.ds(pl.multiple_of(slot * rows, rows), rows)

    own = []
    for part, source in enumerate((key_hbm, value_hbm)):
        for g in range(chunks):
            own.append(
                pltpu.make_async_copy(
                    source.at[:, pl.ds(g * CHUNK, CHUNK)],
                    kv.at[g, part, pl.ds(REACH * rows, rows), :],
                    own_sem.at[g, part],
                )
            )
    local = [
        pltpu.make_async_copy(source, target, local_sem.at[i])
        for i, (source, target) in enumerate(
            (
                (lengths_hbm, lengths),
                (table_hbm, table),
                (bucket_bias_hbm, bucket_bias),
                (query_hbm, query),
                (frames_hbm, frames),
                (out_w_hbm, out_w),
                (norm_gain_hbm, norm_gain),
                (expand_hbm, expand),
                (taps_hbm, taps),
                (inner_gain_hbm, inner_gain),
                (shrink_hbm, shrink),
            )
        )
    ]

    barrier = pltpu.get_barrier_semaphore()

    def greet(device):
        pl.semaphore_signal(
            barrier, inc=1, device_id={"seq": device}, device_id_type=pl.DeviceIdType.MESH
        )

    greet(partner)
    greet(y_peer)
    pl.when(z_sends)(lambda: greet(z_to))
    pl.when(z_gets)(lambda: greet(z_from))
    pl.when(beside_is)(lambda: greet(beside))
    for copy in local[:4] + own:
        copy.start()
    greetings = (
        2 + z_sends.astype(jnp.int32) + z_gets.astype(jnp.int32) + beside_is.astype(jnp.int32)
    )
    pl.semaphore_wait(barrier, greetings)

    def remote(source, target, send, recv, device):
        return pltpu.make_async_remote_copy(
            src_ref=source,
            dst_ref=target,
            send_sem=send,
            recv_sem=recv,
            device_id={"seq": device},
            device_id_type=pl.DeviceIdType.MESH,
        )

    def own_copy(g, part, slot, send, recv, device):
        source = (key_hbm, value_hbm)[part]
        return remote(
            source.at[:, pl.ds(g * CHUNK, CHUNK)],
            kv.at[g, part, slot_rows(slot), :],
            send.at[g, part],
            recv.at[g, part],
            device,
        )

    def relay(g, part, from_slot, to_slot, send, recv, device):
        return remote(
            kv.at[g, part, slot_rows(from_slot), :],
            kv.at[g, part, slot_rows(to_slot), :],
            send.at[g, part],
            recv.at[g, part],
            device,
        )

    def y_copy(g, part, slot):
        return own_copy(g, part, slot, y_send, y_recv, y_peer)

    def p_copy(g, part, slot):
        return own_copy(g, part, slot, p_send, p_recv, partner)

    y_target = jnp.where(is_a, 0, 4)
    p_target = 2 * core + 1
    p_slot = 3 - 2 * core
    c_target = jnp.where(core == 0, 3, 1)
    c_source = jnp.where(outer, y_slot, z_slot)

    def z_copy(g, part):
        return relay(g, part, y_slot, z_slot, z_send, z_recv, z_to)

    def c_copy(g, part, target):
        return relay(g, part, c_source, target, c_send, c_recv, partner)

    pieces = [(g, part) for part in range(2) for g in range(chunks)]

    def send_own(g, part):
        y_copy(g, part, y_target).start()
        p_copy(g, part, p_target).start()

    for piece in pieces[:IN_FLIGHT]:
        send_own(*piece)

    @pl.when(jnp.logical_not(z_gets))
    def _():
        for g in range(chunks):
            kv[g, :, slot_rows(z_slot), :] = jnp.zeros((2, rows, CHUNK), kv.dtype)

    @pl.when(jnp.logical_not(c_gets))
    def _():
        for g in range(chunks):
            kv[g, :, slot_rows(c_slot), :] = jnp.zeros((2, rows, CHUNK), kv.dtype)

    zero_halo = jnp.zeros((HALO, width), gated.dtype)

    @pl.when(me == 0)
    def _():
        gated[0:HALO, :] = zero_halo

    @pl.when(me == seq_count - 1)
    def _():
        gated[HALO + rows : 2 * HALO + rows, :] = zero_halo

    for copy in local[:3]:
        copy.wait()

    query_at = me * rows + lax.broadcasted_iota(jnp.int32, (rows, 1), 0)
    key_at = (me - REACH) * rows + lax.broadcasted_iota(jnp.int32, (1, window), 1)

    def count(u, state):
        bound, query_seg, key_seg = state
        bound = bound + lengths[u]
        return (
            bound,
            query_seg + (query_at >= bound).astype(jnp.int32),
            key_seg + (key_at >= bound).astype(jnp.int32),
        )

    utterances = lengths.shape[0]
    _, query_seg, key_seg = lax.fori_loop(
        0,
        utterances,
        count,
        (jnp.int32(0), jnp.zeros((rows, 1), jnp.int32), jnp.zeros((1, window), jnp.int32)),
        unroll=utterances <= 32,
    )
    key_seg = jnp.where(key_at < 0, -1, key_seg)

    line_length = table.shape[0]
    padded_length = window + rows
    table_pad[...] = jnp.zeros_like(table_pad)
    table_pad[:, 0:line_length] = table[...].reshape(1, line_length)
    buckets = bucket_bias.shape[1]
    hits = (
        lax.broadcasted_iota(jnp.int32, (buckets, padded_length), 0) == table_pad[...]
    ).astype(jnp.float32)
    bias_line = jnp.dot(
        bucket_bias[...],
        hits,
        precision=lax.Precision.HIGHEST,
        preferred_element_type=jnp.float32,
    )
    heads_here = CHUNK // head_width

    def make_bias(g):
        same = query_seg == key_seg
        for h in range(heads_here):
            head = g * heads_here + h
            line = jnp.broadcast_to(bias_line[head : head + 1, :], (8, padded_length))
            skewed = pltpu.roll(line, padded_length - (rows - 1), 1, stride=1, stride_axis=0)
            for first in range(0, rows, 8):
                block = skewed if first == 0 else pltpu.roll(skewed, first, 1)
                bias[g, h * rows + first : h * rows + first + 8, :] = jnp.where(
                    same[first : first + 8], block[:, :window], masked_score
                )

    head_of_lane = lax.broadcasted_iota(jnp.int32, (rows, CHUNK), 1) // head_width

    def arrive(g, part):
        own[part * chunks + g].wait()
        p_copy(g, part, p_slot).wait_recv()
        pl.when(c_gets)(c_copy(g, part, c_slot).wait_recv)

    def weigh(g):
        chunk_query = query[:, g * CHUNK : (g + 1) * CHUNK]
        stacked = jnp.concatenate(
            [
                jnp.where(head_of_lane == h, chunk_query, jnp.zeros_like(chunk_query))
                for h in range(heads_here)
            ],
            axis=0,
        )
        scores = lax.dot_general(
            stacked, kv[g, 0], (((1,), (1,)), ((), ())), preferred_element_type=jnp.float32
        )
        scores = scores * (head_width**-0.5) + bias[g]
        top = jnp.max(scores, axis=1, keepdims=True)
        weights[g] = jnp.exp(scores - top).astype(jnp.bfloat16)

    def attend(g):
        values_and_ones = jnp.concatenate([kv[g, 1], jnp.ones_like(kv[g, 1])], axis=1)
        weighted = jnp.dot(weights[g], values_and_ones, preferred_element_type=jnp.float32)
        normal = (weighted[:, :CHUNK] / weighted[:, CHUNK:]).astype(jnp.bfloat16)
        chosen = normal[0:rows]
        for h in range(1, heads_here):
            chosen = jnp.where(head_of_lane == h, normal[h * rows : (h + 1) * rows], chosen)
        attended[:, g * CHUNK : (g + 1) * CHUNK] = chosen

    def use(g, part):
        arrive(g, part)
        (weigh, attend)[part](g)

    def pass_y(g, part):
        y_copy(g, part, y_slot).wait_recv()
        pl.when(z_sends)(z_copy(g, part).start)
        pl.when(outer)(c_copy(g, part, c_target).start)

    def pass_z(g, part):
        @pl.when(z_gets)
        def _():
            relay(g, part, y_slot, z_slot, z_send, z_recv, z_to).wait_recv()

        @pl.when(jnp.logical_and(z_gets, jnp.logical_not(outer)))
        def _():
            c_copy(g, part, c_target).start()

    half_att = att_width // 2

    def project(half):
        part = slice(half * half_att, (half + 1) * half_att)
        return jnp.dot(attended[:, part], out_w[part, :], preferred_element_type=jnp.float32)

    local[3].wait()
    make_bias(0)
    make_bias(1)
    for step, (g, part) in enumerate(pieces):
        pass_y(g, part)
        if step + IN_FLIGHT < len(pieces):
            send_own(*pieces[step + IN_FLIGHT])
        for copy in local[4 + step : 5 + step]:
            copy.start()
        if step >= 1:
            pass_z(*pieces[step - 1])
        if part == 0 and g + 2 < chunks:
            make_bias(g + 2)
        if step >= 2:
            use(*pieces[step - 2])
    use(*pieces[-2])
    for copy in local[4:7]:
        copy.wait()
    conv[...] = frames[...].astype(jnp.float32) + project(0)
    pass_z(*pieces[-1])
    use(*pieces[-1])

    mid = (conv[...] + project(1)).astype(jnp.bfloat16)
    frames[...] = mid
    normed = layer_norm(mid.astype(jnp.float32), norm_gain[...]).astype(jnp.bfloat16)
    local[7].wait()

    def to_prev(j):
        cols = pl.ds(j * GATE_COLS, GATE_COLS)
        return remote(
            gated.at[pl.ds(HALO, HALO), cols],
            gated.at[pl.ds(HALO + rows, HALO), cols],
            h_send.at[0, j],
            h_recv.at[0, j],
            me - 1,
        )

    def to_next(j):
        cols = pl.ds(j * GATE_COLS, GATE_COLS)
        return remote(
            gated.at[pl.ds(rows, HALO), cols],
            gated.at[pl.ds(0, HALO), cols],
            h_send.at[1, j],
            h_recv.at[1, j],
            me + 1,
        )

    has_prev = me > 0
    has_next = me < seq_count - 1
    for j in range(gate_chunks):
        first = j * GATE_COLS
        cols = slice(first, first + GATE_COLS)
        linear = jnp.dot(normed, expand[:, cols], preferred_element_type=jnp.float32)
        gate = jnp.dot(
            normed,
            expand[:, width + first : width + first + GATE_COLS],
            preferred_element_type=jnp.float32,
        )
        units = (linear * jax.nn.sigmoid(gate)).astype(jnp.bfloat16)
        gated[HALO : HALO + rows, cols] = units
        pl.when(has_prev)(lambda j=j: to_prev(j).start())
        pl.when(has_next)(lambda j=j: to_next(j).start())
        wide = units.astype(jnp.float32)
        plain[HALO : HALO + rows, cols] = wide
        offset4[HALO - 4 : HALO - 4 + rows, cols] = wide

    local[8].wait()

    def first_row(i, t):
        return i * CONV_ROWS + HALO + DILATION * (t - KERNEL // 2)

    def is_own(i, t):
        return first_row(i, t) >= HALO and first_row(i, t) + CONV_ROWS <= HALO + rows

    def add_taps(total, i, cols, chosen):
        for t in chosen:
            row = first_row(i, t)
            source = plain if row % 8 == 0 else offset4
            row -= row % 8
            term = taps[t : t + 1, cols] * source[row : row + CONV_ROWS, cols]
            total = term if total is None else total + term
        return total

    tiles = [
        (i, slice(c * CONV_COLS, (c + 1) * CONV_COLS))
        for c in range(width // CONV_COLS)
        for i in range(rows // CONV_ROWS)
    ]
    for i, cols in tiles:
        conv[i * CONV_ROWS : (i + 1) * CONV_ROWS, cols] = add_taps(
            None, i, cols, [t for t in range(KERNEL) if is_own(i, t)]
        )

    for c in range(width // CONV_COLS):
        half = slice(c * CONV_COLS, (c + 1) * CONV_COLS)
        for j in range(half.start // GATE_COLS, half.stop // GATE_COLS):
            pl.when(has_next)(lambda j=j: to_prev(j).wait_recv())
            pl.when(has_prev)(lambda j=j: to_next(j).wait_recv())
        left = gated[0:HALO, half].astype(jnp.float32)
        right = gated[HALO + rows : 2 * HALO + rows, half].astype(jnp.float32)
        plain[0:HALO, half] = left
        plain[HALO + rows : 2 * HALO + rows, half] = right
        offset4[0 : HALO - 4, half] = left[4:HALO]
        offset4[HALO - 4 + rows : 2 * HALO - 4 + rows, half] = right
        for i in range(rows // CONV_ROWS):
            here = slice(i * CONV_ROWS, (i + 1) * CONV_ROWS)
            conv[here, half] = add_taps(
                conv[here, half], i, half, [t for t in range(KERNEL) if not is_own(i, t)]
            )

    local[9].wait()
    inner = layer_norm(conv[...], inner_gain[...])
    activated = (inner * jax.nn.sigmoid(inner)).astype(jnp.bfloat16)
    local[10].wait()
    leaving = []
    for j in range(gate_chunks):
        cols = slice(j * GATE_COLS, (j + 1) * GATE_COLS)
        result[:, cols] = (
            frames[:, cols].astype(jnp.float32)
            + jnp.dot(activated, shrink[:, cols], preferred_element_type=jnp.float32)
        ).astype(jnp.bfloat16)
        leaving.append(
            pltpu.make_async_copy(result.at[:, cols], out.at[:, cols], out_sem.at[j])
        )
        leaving[j].start()

    for g in range(chunks):
        for part in range(2):
            y_copy(g, part, y_target).wait_send()
            p_copy(g, part, p_target).wait_send()
            pl.when(z_sends)(z_copy(g, part).wait_send)
            pl.when(c_sends)(c_copy(g, part, c_target).wait_send)
    for j in range(gate_chunks):
        pl.when(has_prev)(lambda j=j: to_prev(j).wait_send())
        pl.when(has_next)(lambda j=j: to_next(j).wait_send())
    for copy in leaving:
        copy.wait()


def hand_over(source, target, held, in_sems, out_sems):
    count = in_sems.shape[0]
    part_rows = source.shape[0] // count
    parts = [pl.ds(i * part_rows, part_rows) for i in range(count)]
    inward = [
        pltpu.make_async_copy(source.at[part, :], held.at[part, :], in_sems.at[i])
        for i, part in enumerate(parts)
    ]
    outward = [
        pltpu.make_async_copy(held.at[part, :], target.at[part, :], out_sems.at[i])
        for i, part in enumerate(parts)
    ]
    for copy in inward:
        copy.start()
    for first, second in zip(inward, outward):
        first.wait()
        second.start()
    for copy in outward:
        copy.wait()


def on_device(
    frames_in,
    query_proj,
    key_proj,
    value_proj,
    utterance_lengths,
    bucket_table,
    bucket_bias,
    out_weight,
    norm_gain,
    expand_weight,
    depth_taps,
    inner_gain,
    shrink_weight,
):
    rows, width = frames_in.shape
    att_width = query_proj.shape[1]
    chunks = att_width // CHUNK
    gate_chunks = width // GATE_COLS
    window = SLOTS * rows
    heads_here = CHUNK // (att_width // bucket_bias.shape[1])
    wide_rows = rows + 2 * HALO
    bf16, f32 = jnp.bfloat16, jnp.float32
    anywhere = pl.BlockSpec(memory_space=pl.ANY)
    dma = pltpu.SemaphoreType.DMA
    block_out = pl.pallas_call(
        functools.partial(kernel, lax.axis_size("seq")),
        out_shape=jax.ShapeDtypeStruct((rows, width), bf16),
        in_specs=[anywhere] * 13,
        out_specs=anywhere,
        scratch_shapes=[
            pltpu.SMEM(utterance_lengths.shape, jnp.int32),
            pltpu.VMEM(bucket_table.shape, jnp.int32),
            pltpu.VMEM(bucket_bias.shape[::-1], f32),
            pltpu.VMEM((1, width), f32),
            pltpu.VMEM((1, width), f32),
            pltpu.VMEM((rows, width), bf16),
            pltpu.VMEM((rows, att_width), bf16),
            pltpu.VMEM(out_weight.shape, bf16),
            pltpu.VMEM(expand_weight.shape, bf16),
            pltpu.VMEM(depth_taps.shape, f32),
            pltpu.VMEM(shrink_weight.shape, bf16),
            pltpu.VMEM((chunks, 2, window, CHUNK), bf16),
            pltpu.VMEM((1, window + rows), jnp.int32),
            pltpu.VMEM((chunks, heads_here * rows, window), f32),
            pltpu.VMEM((rows, att_width), bf16),
            pltpu.VMEM((wide_rows, width), bf16),
            pltpu.VMEM((wide_rows, width), f32),
            pltpu.VMEM((wide_rows, width), f32),
            pltpu.VMEM((rows, width), f32),
            pltpu.VMEM((rows, width), bf16),
            pltpu.VMEM((chunks, heads_here * rows, window), bf16),
            dma((11,)),
            dma((chunks, 2)),
            dma((chunks, 2)),
            dma((chunks, 2)),
            dma((chunks, 2)),
            dma((chunks, 2)),
            dma((chunks, 2)),
            dma((chunks, 2)),
            dma((chunks, 2)),
            dma((chunks, 2)),
            dma((2, gate_chunks)),
            dma((2, gate_chunks)),
            dma((gate_chunks,)),
        ],
        compiler_params=pltpu.CompilerParams(
            collective_id=0, has_side_effects=True, vmem_limit_bytes=60 * 1024 * 1024
        ),
    )(
        utterance_lengths,
        bucket_table,
        bucket_bias.T,
        norm_gain.reshape(1, -1),
        inner_gain.reshape(1, -1),
        frames_in,
        query_proj,
        key_proj,
        value_proj,
        out_weight,
        expand_weight,
        depth_taps,
        shrink_weight,
    )
    return pl.pallas_call(
        hand_over,
        out_shape=jax.ShapeDtypeStruct((rows, width), bf16),
        in_specs=[anywhere],
        out_specs=anywhere,
        scratch_shapes=[pltpu.VMEM((rows, width), bf16), dma((4,)), dma((4,))],
        compiler_params=pltpu.CompilerParams(vmem_limit_bytes=60 * 1024 * 1024),
    )(block_out)


def solution(mesh):
    placed = (
        P(("groups", "seq"), None),
        P(("groups", "seq"), None),
        P(("groups", "seq"), None),
        P(("groups", "seq"), None),
        P("groups"),
        P(),
        P(),
        P(),
        P(),
        P(),
        P(),
        P(),
        P(),
    )
    return jax.shard_map(
        on_device, mesh=mesh, in_specs=placed, out_specs=P(("groups", "seq"), None), check_vma=False
    )
```

```python
import functools

import jax
import jax.numpy as jnp
from jax import lax
from jax.experimental import pallas as pl
from jax.experimental.pallas import tpu as pltpu
from jax.sharding import PartitionSpec as P

KERNEL = 31
DILATION = 4
REACH = 2
SLOTS = 2 * REACH + 1
CHUNK = 128
GATE_COLS = 256
HALO = 64
Z_LAG = 3
USE_LAG = 5
CONV_ROWS = 32
CONV_COLS = 512

norm_epsilon = 1e-05
masked_score = -1e30


def layer_norm(values, gain_vec):
    row_mean = jnp.mean(values, axis=-1, keepdims=True)
    centred = values - row_mean
    spread = jnp.mean(centred * centred, axis=-1, keepdims=True)
    return centred * lax.rsqrt(spread + norm_epsilon) * gain_vec


def kernel(
    seq_count,
    lengths_hbm,
    table_hbm,
    bucket_bias_hbm,
    norm_gain_hbm,
    inner_gain_hbm,
    frames_hbm,
    query_hbm,
    key_hbm,
    value_hbm,
    out_w_hbm,
    expand_hbm,
    taps_hbm,
    shrink_hbm,
    out,
    lengths,
    table,
    bucket_bias,
    norm_gain,
    inner_gain,
    frames,
    query,
    out_w,
    expand,
    taps,
    shrink,
    kv,
    table_pad,
    bias,
    attended,
    gated,
    plain,
    offset4,
    conv,
    result,
    weights,
    local_sem,
    own_sem,
    p_send,
    p_recv,
    y_send,
    y_recv,
    z_send,
    z_recv,
    c_send,
    c_recv,
    h_send,
    h_recv,
    out_sem,
):
    rows, width = frames.shape
    att_width = query.shape[1]
    chunks = att_width // CHUNK
    head_width = att_width // bucket_bias.shape[0]
    window = SLOTS * rows
    gate_chunks = width // GATE_COLS

    me = lax.axis_index("seq")
    core = lax.rem(me, 2)
    is_a = lax.rem(me, 4) < 2
    outer = is_a == (core == 0)
    partner = me + 1 - 2 * core
    y_peer = jnp.where(is_a, me + 2, me - 2)
    z_to = jnp.where(is_a, me + 4, me - 4)
    z_from = jnp.where(is_a, me - 4, me + 4)
    beside = jnp.where(core == 0, me - 1, me + 1)
    z_sends = jnp.logical_and(z_to >= 0, z_to < seq_count)
    z_gets = jnp.logical_and(z_from >= 0, z_from < seq_count)
    beside_is = jnp.logical_and(beside >= 0, beside < seq_count)
    c_sends = jnp.logical_or(outer, z_gets)
    c_gets = jnp.logical_or(jnp.logical_not(outer), z_gets)
    y_slot = jnp.where(is_a, 4, 0)
    z_slot = jnp.where(is_a, 0, 4)
    c_slot = jnp.where(core == 0, 1, 3)

    def slot_rows(slot):
        return pl.ds(pl.multiple_of(slot * rows, rows), rows)

    own = []
    for part, source in enumerate((key_hbm, value_hbm)):
        for g in range(chunks):
            own.append(
                pltpu.make_async_copy(
                    source.at[:, pl.ds(g * CHUNK, CHUNK)],
                    kv.at[g, part, pl.ds(REACH * rows, rows), :],
                    own_sem.at[g, part],
                )
            )
    local = [
        pltpu.make_async_copy(source, target, local_sem.at[i])
        for i, (source, target) in enumerate(
            (
                (lengths_hbm, lengths),
                (table_hbm, table),
                (bucket_bias_hbm, bucket_bias),
                (query_hbm, query),
                (frames_hbm, frames),
                (out_w_hbm, out_w),
                (norm_gain_hbm, norm_gain),
                (expand_hbm, expand),
                (taps_hbm, taps),
                (inner_gain_hbm, inner_gain),
                (shrink_hbm, shrink),
            )
        )
    ]

    barrier = pltpu.get_barrier_semaphore()

    def greet(device):
        pl.semaphore_signal(
            barrier, inc=1, device_id={"seq": device}, device_id_type=pl.DeviceIdType.MESH
        )

    greet(partner)
    greet(y_peer)
    pl.when(z_sends)(lambda: greet(z_to))
    pl.when(z_gets)(lambda: greet(z_from))
    pl.when(beside_is)(lambda: greet(beside))
    for copy in local[:4] + own:
        copy.start()
    greetings = (
        2 + z_sends.astype(jnp.int32) + z_gets.astype(jnp.int32) + beside_is.astype(jnp.int32)
    )
    pl.semaphore_wait(barrier, greetings)

    def remote(source, target, send, recv, device):
        return pltpu.make_async_remote_copy(
            src_ref=source,
            dst_ref=target,
            send_sem=send,
            recv_sem=recv,
            device_id={"seq": device},
            device_id_type=pl.DeviceIdType.MESH,
        )

    def own_copy(g, part, slot, send, recv, device):
        source = (key_hbm, value_hbm)[part]
        return remote(
            source.at[:, pl.ds(g * CHUNK, CHUNK)],
            kv.at[g, part, slot_rows(slot), :],
            send.at[g, part],
            recv.at[g, part],
            device,
        )

    def relay(g, part, from_slot, to_slot, send, recv, device):
        return remote(
            kv.at[g, part, slot_rows(from_slot), :],
            kv.at[g, part, slot_rows(to_slot), :],
            send.at[g, part],
            recv.at[g, part],
            device,
        )

    def y_copy(g, part, slot):
        return own_copy(g, part, slot, y_send, y_recv, y_peer)

    def p_copy(g, part, slot):
        return own_copy(g, part, slot, p_send, p_recv, partner)

    y_target = jnp.where(is_a, 0, 4)
    p_target = 2 * core + 1
    p_slot = 3 - 2 * core
    c_target = jnp.where(core == 0, 3, 1)
    c_source = jnp.where(outer, y_slot, z_slot)

    def z_copy(g, part):
        return relay(g, part, y_slot, z_slot, z_send, z_recv, z_to)

    def c_copy(g, part, target):
        return relay(g, part, c_source, target, c_send, c_recv, partner)

    pieces = [(g, part) for part in range(2) for g in range(chunks)]

    def send_own(g, part):
        y_copy(g, part, y_target).start()
        p_copy(g, part, p_target).start()

    for piece in pieces:
        send_own(*piece)

    @pl.when(jnp.logical_not(z_gets))
    def _():
        for g in range(chunks):
            kv[g, :, slot_rows(z_slot), :] = jnp.zeros((2, rows, CHUNK), kv.dtype)

    @pl.when(jnp.logical_not(c_gets))
    def _():
        for g in range(chunks):
            kv[g, :, slot_rows(c_slot), :] = jnp.zeros((2, rows, CHUNK), kv.dtype)

    zero_halo = jnp.zeros((HALO, width), gated.dtype)

    @pl.when(me == 0)
    def _():
        gated[0:HALO, :] = zero_halo

    @pl.when(me == seq_count - 1)
    def _():
        gated[HALO + rows : 2 * HALO + rows, :] = zero_halo

    for copy in local[:3]:
        copy.wait()

    query_at = me * rows + lax.broadcasted_iota(jnp.int32, (rows, 1), 0)
    key_at = (me - REACH) * rows + lax.broadcasted_iota(jnp.int32, (1, window), 1)

    def count(u, state):
        bound, query_seg, key_seg = state
        bound = bound + lengths[u]
        return (
            bound,
            query_seg + (query_at >= bound).astype(jnp.int32),
            key_seg + (key_at >= bound).astype(jnp.int32),
        )

    utterances = lengths.shape[0]
    _, query_seg, key_seg = lax.fori_loop(
        0,
        utterances,
        count,
        (jnp.int32(0), jnp.zeros((rows, 1), jnp.int32), jnp.zeros((1, window), jnp.int32)),
        unroll=utterances <= 32,
    )
    key_seg = jnp.where(key_at < 0, -1, key_seg)

    line_length = table.shape[0]
    padded_length = window + rows
    table_pad[...] = jnp.zeros_like(table_pad)
    table_pad[:, 0:line_length] = table[...].reshape(1, line_length)
    buckets = bucket_bias.shape[1]
    hits = (
        lax.broadcasted_iota(jnp.int32, (buckets, padded_length), 0) == table_pad[...]
    ).astype(jnp.float32)
    bias_line = jnp.dot(
        bucket_bias[...],
        hits,
        precision=lax.Precision.HIGHEST,
        preferred_element_type=jnp.float32,
    )
    heads_here = CHUNK // head_width

    def make_bias(g):
        same = query_seg == key_seg
        for h in range(heads_here):
            head = g * heads_here + h
            line = jnp.broadcast_to(bias_line[head : head + 1, :], (8, padded_length))
            skewed = pltpu.roll(line, padded_length - (rows - 1), 1, stride=1, stride_axis=0)
            for first in range(0, rows, 8):
                block = skewed if first == 0 else pltpu.roll(skewed, first, 1)
                bias[g, h * rows + first : h * rows + first + 8, :] = jnp.where(
                    same[first : first + 8], block[:, :window], masked_score
                )

    head_of_lane = lax.broadcasted_iota(jnp.int32, (rows, CHUNK), 1) // head_width

    def arrive(g, part):
        own[part * chunks + g].wait()
        p_copy(g, part, p_slot).wait_recv()
        pl.when(c_gets)(c_copy(g, part, c_slot).wait_recv)

    def weigh(g):
        chunk_query = query[:, g * CHUNK : (g + 1) * CHUNK]
        stacked = jnp.concatenate(
            [
                jnp.where(head_of_lane == h, chunk_query, jnp.zeros_like(chunk_query))
                for h in range(heads_here)
            ],
            axis=0,
        )
        scores = lax.dot_general(
            stacked, kv[g, 0], (((1,), (1,)), ((), ())), preferred_element_type=jnp.float32
        )
        scores = scores * (head_width**-0.5) + bias[g]
        top = jnp.max(scores, axis=1, keepdims=True)
        weights[g] = jnp.exp(scores - top).astype(jnp.bfloat16)

    def attend(g):
        values_and_ones = jnp.concatenate([kv[g, 1], jnp.ones_like(kv[g, 1])], axis=1)
        weighted = jnp.dot(weights[g], values_and_ones, preferred_element_type=jnp.float32)
        normal = (weighted[:, :CHUNK] / weighted[:, CHUNK:]).astype(jnp.bfloat16)
        chosen = normal[0:rows]
        for h in range(1, heads_here):
            chosen = jnp.where(head_of_lane == h, normal[h * rows : (h + 1) * rows], chosen)
        attended[:, g * CHUNK : (g + 1) * CHUNK] = chosen

    def use(g, part):
        arrive(g, part)
        (weigh, attend)[part](g)

    def pass_y(g, part):
        y_copy(g, part, y_slot).wait_recv()
        pl.when(z_sends)(z_copy(g, part).start)
        pl.when(outer)(c_copy(g, part, c_target).start)

    def pass_z(g, part):
        @pl.when(z_gets)
        def _():
            relay(g, part, y_slot, z_slot, z_send, z_recv, z_to).wait_recv()

        @pl.when(jnp.logical_and(z_gets, jnp.logical_not(outer)))
        def _():
            c_copy(g, part, c_target).start()

    half_att = att_width // 2

    def project(half):
        part = slice(half * half_att, (half + 1) * half_att)
        return jnp.dot(attended[:, part], out_w[part, :], preferred_element_type=jnp.float32)

    local[3].wait()
    make_bias(0)
    make_bias(1)
    count_of = len(pieces)
    for step in range(count_of + USE_LAG):
        if step < count_of:
            pass_y(*pieces[step])
        for copy in local[4 + step : 5 + step]:
            copy.start()
        if 0 <= step - Z_LAG < count_of:
            pass_z(*pieces[step - Z_LAG])
        if step + 2 < chunks:
            make_bias(step + 2)
        if step == count_of + USE_LAG - 1:
            for copy in local[4:7]:
                copy.wait()
            conv[...] = frames[...].astype(jnp.float32) + project(0)
        if step >= USE_LAG:
            use(*pieces[step - USE_LAG])

    mid = (conv[...] + project(1)).astype(jnp.bfloat16)
    frames[...] = mid
    normed = layer_norm(mid.astype(jnp.float32), norm_gain[...]).astype(jnp.bfloat16)
    local[7].wait()

    def to_prev(j):
        cols = pl.ds(j * GATE_COLS, GATE_COLS)
        return remote(
            gated.at[pl.ds(HALO, HALO), cols],
            gated.at[pl.ds(HALO + rows, HALO), cols],
            h_send.at[0, j],
            h_recv.at[0, j],
            me - 1,
        )

    def to_next(j):
        cols = pl.ds(j * GATE_COLS, GATE_COLS)
        return remote(
            gated.at[pl.ds(rows, HALO), cols],
            gated.at[pl.ds(0, HALO), cols],
            h_send.at[1, j],
            h_recv.at[1, j],
            me + 1,
        )

    has_prev = me > 0
    has_next = me < seq_count - 1
    for j in range(gate_chunks):
        first = j * GATE_COLS
        cols = slice(first, first + GATE_COLS)
        linear = jnp.dot(normed, expand[:, cols], preferred_element_type=jnp.float32)
        gate = jnp.dot(
            normed,
            expand[:, width + first : width + first + GATE_COLS],
            preferred_element_type=jnp.float32,
        )
        units = (linear * jax.nn.sigmoid(gate)).astype(jnp.bfloat16)
        gated[HALO : HALO + rows, cols] = units
        pl.when(has_prev)(lambda j=j: to_prev(j).start())
        pl.when(has_next)(lambda j=j: to_next(j).start())
        wide = units.astype(jnp.float32)
        plain[HALO : HALO + rows, cols] = wide
        offset4[HALO - 4 : HALO - 4 + rows, cols] = wide

    local[8].wait()

    def first_row(i, t):
        return i * CONV_ROWS + HALO + DILATION * (t - KERNEL // 2)

    def is_own(i, t):
        return first_row(i, t) >= HALO and first_row(i, t) + CONV_ROWS <= HALO + rows

    def add_taps(total, i, cols, chosen):
        for t in chosen:
            row = first_row(i, t)
            source = plain if row % 8 == 0 else offset4
            row -= row % 8
            term = taps[t : t + 1, cols] * source[row : row + CONV_ROWS, cols]
            total = term if total is None else total + term
        return total

    tiles = [
        (i, slice(c * CONV_COLS, (c + 1) * CONV_COLS))
        for c in range(width // CONV_COLS)
        for i in range(rows // CONV_ROWS)
    ]
    for i, cols in tiles:
        conv[i * CONV_ROWS : (i + 1) * CONV_ROWS, cols] = add_taps(
            None, i, cols, [t for t in range(KERNEL) if is_own(i, t)]
        )

    for c in range(width // CONV_COLS):
        half = slice(c * CONV_COLS, (c + 1) * CONV_COLS)
        for j in range(half.start // GATE_COLS, half.stop // GATE_COLS):
            pl.when(has_next)(lambda j=j: to_prev(j).wait_recv())
            pl.when(has_prev)(lambda j=j: to_next(j).wait_recv())
        left = gated[0:HALO, half].astype(jnp.float32)
        right = gated[HALO + rows : 2 * HALO + rows, half].astype(jnp.float32)
        plain[0:HALO, half] = left
        plain[HALO + rows : 2 * HALO + rows, half] = right
        offset4[0 : HALO - 4, half] = left[4:HALO]
        offset4[HALO - 4 + rows : 2 * HALO - 4 + rows, half] = right
        for i in range(rows // CONV_ROWS):
            here = slice(i * CONV_ROWS, (i + 1) * CONV_ROWS)
            conv[here, half] = add_taps(
                conv[here, half], i, half, [t for t in range(KERNEL) if not is_own(i, t)]
            )

    local[9].wait()
    inner = layer_norm(conv[...], inner_gain[...])
    activated = (inner * jax.nn.sigmoid(inner)).astype(jnp.bfloat16)
    local[10].wait()
    leaving = []
    for j in range(gate_chunks):
        cols = slice(j * GATE_COLS, (j + 1) * GATE_COLS)
        result[:, cols] = (
            frames[:, cols].astype(jnp.float32)
            + jnp.dot(activated, shrink[:, cols], preferred_element_type=jnp.float32)
        ).astype(jnp.bfloat16)
        leaving.append(
            pltpu.make_async_copy(result.at[:, cols], out.at[:, cols], out_sem.at[j])
        )
        leaving[j].start()

    for g in range(chunks):
        for part in range(2):
            y_copy(g, part, y_target).wait_send()
            p_copy(g, part, p_target).wait_send()
            pl.when(z_sends)(z_copy(g, part).wait_send)
            pl.when(c_sends)(c_copy(g, part, c_target).wait_send)
    for j in range(gate_chunks):
        pl.when(has_prev)(lambda j=j: to_prev(j).wait_send())
        pl.when(has_next)(lambda j=j: to_next(j).wait_send())
    for copy in leaving:
        copy.wait()


def hand_over(source, target, held, in_sems, out_sems):
    count = in_sems.shape[0]
    part_rows = source.shape[0] // count
    parts = [pl.ds(i * part_rows, part_rows) for i in range(count)]
    inward = [
        pltpu.make_async_copy(source.at[part, :], held.at[part, :], in_sems.at[i])
        for i, part in enumerate(parts)
    ]
    outward = [
        pltpu.make_async_copy(held.at[part, :], target.at[part, :], out_sems.at[i])
        for i, part in enumerate(parts)
    ]
    for copy in inward:
        copy.start()
    for first, second in zip(inward, outward):
        first.wait()
        second.start()
    for copy in outward:
        copy.wait()


def on_device(
    frames_in,
    query_proj,
    key_proj,
    value_proj,
    utterance_lengths,
    bucket_table,
    bucket_bias,
    out_weight,
    norm_gain,
    expand_weight,
    depth_taps,
    inner_gain,
    shrink_weight,
):
    rows, width = frames_in.shape
    att_width = query_proj.shape[1]
    chunks = att_width // CHUNK
    gate_chunks = width // GATE_COLS
    window = SLOTS * rows
    heads_here = CHUNK // (att_width // bucket_bias.shape[1])
    wide_rows = rows + 2 * HALO
    bf16, f32 = jnp.bfloat16, jnp.float32
    anywhere = pl.BlockSpec(memory_space=pl.ANY)
    dma = pltpu.SemaphoreType.DMA
    block_out = pl.pallas_call(
        functools.partial(kernel, lax.axis_size("seq")),
        out_shape=jax.ShapeDtypeStruct((rows, width), bf16),
        in_specs=[anywhere] * 13,
        out_specs=anywhere,
        scratch_shapes=[
            pltpu.SMEM(utterance_lengths.shape, jnp.int32),
            pltpu.VMEM(bucket_table.shape, jnp.int32),
            pltpu.VMEM(bucket_bias.shape[::-1], f32),
            pltpu.VMEM((1, width), f32),
            pltpu.VMEM((1, width), f32),
            pltpu.VMEM((rows, width), bf16),
            pltpu.VMEM((rows, att_width), bf16),
            pltpu.VMEM(out_weight.shape, bf16),
            pltpu.VMEM(expand_weight.shape, bf16),
            pltpu.VMEM(depth_taps.shape, f32),
            pltpu.VMEM(shrink_weight.shape, bf16),
            pltpu.VMEM((chunks, 2, window, CHUNK), bf16),
            pltpu.VMEM((1, window + rows), jnp.int32),
            pltpu.VMEM((chunks, heads_here * rows, window), f32),
            pltpu.VMEM((rows, att_width), bf16),
            pltpu.VMEM((wide_rows, width), bf16),
            pltpu.VMEM((wide_rows, width), f32),
            pltpu.VMEM((wide_rows, width), f32),
            pltpu.VMEM((rows, width), f32),
            pltpu.VMEM((rows, width), bf16),
            pltpu.VMEM((chunks, heads_here * rows, window), bf16),
            dma((11,)),
            dma((chunks, 2)),
            dma((chunks, 2)),
            dma((chunks, 2)),
            dma((chunks, 2)),
            dma((chunks, 2)),
            dma((chunks, 2)),
            dma((chunks, 2)),
            dma((chunks, 2)),
            dma((chunks, 2)),
            dma((2, gate_chunks)),
            dma((2, gate_chunks)),
            dma((gate_chunks,)),
        ],
        compiler_params=pltpu.CompilerParams(
            collective_id=0, has_side_effects=True, vmem_limit_bytes=60 * 1024 * 1024
        ),
    )(
        utterance_lengths,
        bucket_table,
        bucket_bias.T,
        norm_gain.reshape(1, -1),
        inner_gain.reshape(1, -1),
        frames_in,
        query_proj,
        key_proj,
        value_proj,
        out_weight,
        expand_weight,
        depth_taps,
        shrink_weight,
    )
    return pl.pallas_call(
        hand_over,
        out_shape=jax.ShapeDtypeStruct((rows, width), bf16),
        in_specs=[anywhere],
        out_specs=anywhere,
        scratch_shapes=[pltpu.VMEM((rows, width), bf16), dma((4,)), dma((4,))],
        compiler_params=pltpu.CompilerParams(vmem_limit_bytes=60 * 1024 * 1024),
    )(block_out)


def solution(mesh):
    placed = (
        P(("groups", "seq"), None),
        P(("groups", "seq"), None),
        P(("groups", "seq"), None),
        P(("groups", "seq"), None),
        P("groups"),
        P(),
        P(),
        P(),
        P(),
        P(),
        P(),
        P(),
        P(),
    )
    return jax.shard_map(
        on_device, mesh=mesh, in_specs=placed, out_specs=P(("groups", "seq"), None), check_vma=False
    )
```

```python
import functools

import jax
import jax.numpy as jnp
from jax import lax
from jax.experimental import pallas as pl
from jax.experimental.pallas import tpu as pltpu
from jax.sharding import PartitionSpec as P

KERNEL = 31
DILATION = 4
REACH = 2
SLOTS = 2 * REACH + 1
CHUNK = 128
GATE_COLS = 256
HALO = 64
Z_LAG = 4
USE_LAG = 7
CONV_ROWS = 32
CONV_COLS = 512

norm_epsilon = 1e-05
masked_score = -1e30


def layer_norm(values, gain_vec):
    row_mean = jnp.mean(values, axis=-1, keepdims=True)
    centred = values - row_mean
    spread = jnp.mean(centred * centred, axis=-1, keepdims=True)
    return centred * lax.rsqrt(spread + norm_epsilon) * gain_vec


def kernel(
    seq_count,
    lengths_hbm,
    table_hbm,
    bucket_bias_hbm,
    norm_gain_hbm,
    inner_gain_hbm,
    frames_hbm,
    query_hbm,
    key_hbm,
    value_hbm,
    out_w_hbm,
    expand_hbm,
    taps_hbm,
    shrink_hbm,
    out,
    lengths,
    table,
    bucket_bias,
    norm_gain,
    inner_gain,
    frames,
    query,
    out_w,
    expand,
    taps,
    shrink,
    kv,
    table_pad,
    bias,
    attended,
    gated,
    plain,
    offset4,
    conv,
    result,
    weights,
    local_sem,
    own_sem,
    p_send,
    p_recv,
    y_send,
    y_recv,
    z_send,
    z_recv,
    c_send,
    c_recv,
    h_send,
    h_recv,
    out_sem,
):
    rows, width = frames.shape
    att_width = query.shape[1]
    chunks = att_width // CHUNK
    head_width = att_width // bucket_bias.shape[0]
    window = SLOTS * rows
    gate_chunks = width // GATE_COLS

    me = lax.axis_index("seq")
    core = lax.rem(me, 2)
    is_a = lax.rem(me, 4) < 2
    outer = is_a == (core == 0)
    partner = me + 1 - 2 * core
    y_peer = jnp.where(is_a, me + 2, me - 2)
    z_to = jnp.where(is_a, me + 4, me - 4)
    z_from = jnp.where(is_a, me - 4, me + 4)
    beside = jnp.where(core == 0, me - 1, me + 1)
    z_sends = jnp.logical_and(z_to >= 0, z_to < seq_count)
    z_gets = jnp.logical_and(z_from >= 0, z_from < seq_count)
    beside_is = jnp.logical_and(beside >= 0, beside < seq_count)
    c_sends = jnp.logical_or(outer, z_gets)
    c_gets = jnp.logical_or(jnp.logical_not(outer), z_gets)
    y_slot = jnp.where(is_a, 4, 0)
    z_slot = jnp.where(is_a, 0, 4)
    c_slot = jnp.where(core == 0, 1, 3)

    def slot_rows(slot):
        return pl.ds(pl.multiple_of(slot * rows, rows), rows)

    own = []
    for part, source in enumerate((key_hbm, value_hbm)):
        for g in range(chunks):
            own.append(
                pltpu.make_async_copy(
                    source.at[:, pl.ds(g * CHUNK, CHUNK)],
                    kv.at[g, part, pl.ds(REACH * rows, rows), :],
                    own_sem.at[g, part],
                )
            )
    local = [
        pltpu.make_async_copy(source, target, local_sem.at[i])
        for i, (source, target) in enumerate(
            (
                (lengths_hbm, lengths),
                (table_hbm, table),
                (bucket_bias_hbm, bucket_bias),
                (query_hbm, query),
                (frames_hbm, frames),
                (out_w_hbm, out_w),
                (norm_gain_hbm, norm_gain),
                (expand_hbm, expand),
                (taps_hbm, taps),
                (inner_gain_hbm, inner_gain),
                (shrink_hbm, shrink),
            )
        )
    ]

    barrier = pltpu.get_barrier_semaphore()

    def greet(device):
        pl.semaphore_signal(
            barrier, inc=1, device_id={"seq": device}, device_id_type=pl.DeviceIdType.MESH
        )

    greet(partner)
    greet(y_peer)
    pl.when(z_sends)(lambda: greet(z_to))
    pl.when(z_gets)(lambda: greet(z_from))
    pl.when(beside_is)(lambda: greet(beside))
    for copy in local[:4] + own:
        copy.start()
    greetings = (
        2 + z_sends.astype(jnp.int32) + z_gets.astype(jnp.int32) + beside_is.astype(jnp.int32)
    )
    pl.semaphore_wait(barrier, greetings)

    def remote(source, target, send, recv, device):
        return pltpu.make_async_remote_copy(
            src_ref=source,
            dst_ref=target,
            send_sem=send,
            recv_sem=recv,
            device_id={"seq": device},
            device_id_type=pl.DeviceIdType.MESH,
        )

    def own_copy(g, part, slot, send, recv, device):
        source = (key_hbm, value_hbm)[part]
        return remote(
            source.at[:, pl.ds(g * CHUNK, CHUNK)],
            kv.at[g, part, slot_rows(slot), :],
            send.at[g, part],
            recv.at[g, part],
            device,
        )

    def relay(g, part, from_slot, to_slot, send, recv, device):
        return remote(
            kv.at[g, part, slot_rows(from_slot), :],
            kv.at[g, part, slot_rows(to_slot), :],
            send.at[g, part],
            recv.at[g, part],
            device,
        )

    def y_copy(g, part, slot):
        return own_copy(g, part, slot, y_send, y_recv, y_peer)

    def p_copy(g, part, slot):
        return own_copy(g, part, slot, p_send, p_recv, partner)

    y_target = jnp.where(is_a, 0, 4)
    p_target = 2 * core + 1
    p_slot = 3 - 2 * core
    c_target = jnp.where(core == 0, 3, 1)
    c_source = jnp.where(outer, y_slot, z_slot)

    def z_copy(g, part):
        return relay(g, part, y_slot, z_slot, z_send, z_recv, z_to)

    def c_copy(g, part, target):
        return relay(g, part, c_source, target, c_send, c_recv, partner)

    pieces = [(g, part) for part in range(2) for g in range(chunks)]

    def send_own(g, part):
        y_copy(g, part, y_target).start()
        p_copy(g, part, p_target).start()

    for piece in pieces:
        send_own(*piece)

    @pl.when(jnp.logical_not(z_gets))
    def _():
        for g in range(chunks):
            kv[g, :, slot_rows(z_slot), :] = jnp.zeros((2, rows, CHUNK), kv.dtype)

    @pl.when(jnp.logical_not(c_gets))
    def _():
        for g in range(chunks):
            kv[g, :, slot_rows(c_slot), :] = jnp.zeros((2, rows, CHUNK), kv.dtype)

    zero_halo = jnp.zeros((HALO, width), gated.dtype)

    @pl.when(me == 0)
    def _():
        gated[0:HALO, :] = zero_halo

    @pl.when(me == seq_count - 1)
    def _():
        gated[HALO + rows : 2 * HALO + rows, :] = zero_halo

    for copy in local[:3]:
        copy.wait()

    query_at = me * rows + lax.broadcasted_iota(jnp.int32, (rows, 1), 0)
    key_at = (me - REACH) * rows + lax.broadcasted_iota(jnp.int32, (1, window), 1)

    def count(u, state):
        bound, query_seg, key_seg = state
        bound = bound + lengths[u]
        return (
            bound,
            query_seg + (query_at >= bound).astype(jnp.int32),
            key_seg + (key_at >= bound).astype(jnp.int32),
        )

    utterances = lengths.shape[0]
    _, query_seg, key_seg = lax.fori_loop(
        0,
        utterances,
        count,
        (jnp.int32(0), jnp.zeros((rows, 1), jnp.int32), jnp.zeros((1, window), jnp.int32)),
        unroll=utterances <= 32,
    )
    key_seg = jnp.where(key_at < 0, -1, key_seg)

    line_length = table.shape[0]
    padded_length = window + rows
    table_pad[...] = jnp.zeros_like(table_pad)
    table_pad[:, 0:line_length] = table[...].reshape(1, line_length)
    buckets = bucket_bias.shape[1]
    hits = (
        lax.broadcasted_iota(jnp.int32, (buckets, padded_length), 0) == table_pad[...]
    ).astype(jnp.float32)
    bias_line = jnp.dot(
        bucket_bias[...],
        hits,
        precision=lax.Precision.HIGHEST,
        preferred_element_type=jnp.float32,
    )
    heads_here = CHUNK // head_width

    def make_bias(g):
        same = query_seg == key_seg
        for h in range(heads_here):
            head = g * heads_here + h
            line = jnp.broadcast_to(bias_line[head : head + 1, :], (8, padded_length))
            skewed = pltpu.roll(line, padded_length - (rows - 1), 1, stride=1, stride_axis=0)
            for first in range(0, rows, 8):
                block = skewed if first == 0 else pltpu.roll(skewed, first, 1)
                bias[g, h * rows + first : h * rows + first + 8, :] = jnp.where(
                    same[first : first + 8], block[:, :window], masked_score
                )

    head_of_lane = lax.broadcasted_iota(jnp.int32, (rows, CHUNK), 1) // head_width

    def arrive(g, part):
        own[part * chunks + g].wait()
        p_copy(g, part, p_slot).wait_recv()
        pl.when(c_gets)(c_copy(g, part, c_slot).wait_recv)

    def weigh(g):
        chunk_query = query[:, g * CHUNK : (g + 1) * CHUNK]
        stacked = jnp.concatenate(
            [
                jnp.where(head_of_lane == h, chunk_query, jnp.zeros_like(chunk_query))
                for h in range(heads_here)
            ],
            axis=0,
        )
        scores = lax.dot_general(
            stacked, kv[g, 0], (((1,), (1,)), ((), ())), preferred_element_type=jnp.float32
        )
        scores = scores * (head_width**-0.5) + bias[g]
        top = jnp.max(scores, axis=1, keepdims=True)
        weights[g] = jnp.exp(scores - top).astype(jnp.bfloat16)

    def attend(g):
        values_and_ones = jnp.concatenate([kv[g, 1], jnp.ones_like(kv[g, 1])], axis=1)
        weighted = jnp.dot(weights[g], values_and_ones, preferred_element_type=jnp.float32)
        normal = (weighted[:, :CHUNK] / weighted[:, CHUNK:]).astype(jnp.bfloat16)
        chosen = normal[0:rows]
        for h in range(1, heads_here):
            chosen = jnp.where(head_of_lane == h, normal[h * rows : (h + 1) * rows], chosen)
        attended[:, g * CHUNK : (g + 1) * CHUNK] = chosen

    def use(g, part):
        arrive(g, part)
        (weigh, attend)[part](g)

    def pass_y(g, part):
        y_copy(g, part, y_slot).wait_recv()
        pl.when(z_sends)(z_copy(g, part).start)
        pl.when(outer)(c_copy(g, part, c_target).start)

    def pass_z(g, part):
        @pl.when(z_gets)
        def _():
            relay(g, part, y_slot, z_slot, z_send, z_recv, z_to).wait_recv()

        @pl.when(jnp.logical_and(z_gets, jnp.logical_not(outer)))
        def _():
            c_copy(g, part, c_target).start()

    half_att = att_width // 2

    def project(half):
        part = slice(half * half_att, (half + 1) * half_att)
        return jnp.dot(attended[:, part], out_w[part, :], preferred_element_type=jnp.float32)

    local[3].wait()
    make_bias(0)
    make_bias(1)
    count_of = len(pieces)
    for step in range(count_of + USE_LAG):
        if step < count_of:
            pass_y(*pieces[step])
        for copy in local[4 + step : 5 + step]:
            copy.start()
        if 0 <= step - Z_LAG < count_of:
            pass_z(*pieces[step - Z_LAG])
        if step + 2 < chunks:
            make_bias(step + 2)
        if step == count_of + USE_LAG - 1:
            for copy in local[4:7]:
                copy.wait()
            conv[...] = frames[...].astype(jnp.float32) + project(0)
        if step >= USE_LAG:
            use(*pieces[step - USE_LAG])

    mid = (conv[...] + project(1)).astype(jnp.bfloat16)
    frames[...] = mid
    normed = layer_norm(mid.astype(jnp.float32), norm_gain[...]).astype(jnp.bfloat16)
    local[7].wait()

    def to_prev(j):
        cols = pl.ds(j * GATE_COLS, GATE_COLS)
        return remote(
            gated.at[pl.ds(HALO, HALO), cols],
            gated.at[pl.ds(HALO + rows, HALO), cols],
            h_send.at[0, j],
            h_recv.at[0, j],
            me - 1,
        )

    def to_next(j):
        cols = pl.ds(j * GATE_COLS, GATE_COLS)
        return remote(
            gated.at[pl.ds(rows, HALO), cols],
            gated.at[pl.ds(0, HALO), cols],
            h_send.at[1, j],
            h_recv.at[1, j],
            me + 1,
        )

    has_prev = me > 0
    has_next = me < seq_count - 1
    for j in range(gate_chunks):
        first = j * GATE_COLS
        cols = slice(first, first + GATE_COLS)
        linear = jnp.dot(normed, expand[:, cols], preferred_element_type=jnp.float32)
        gate = jnp.dot(
            normed,
            expand[:, width + first : width + first + GATE_COLS],
            preferred_element_type=jnp.float32,
        )
        units = (linear * jax.nn.sigmoid(gate)).astype(jnp.bfloat16)
        gated[HALO : HALO + rows, cols] = units
        pl.when(jnp.logical_and(has_next, core == 1))(to_next(j).start)
        pl.when(has_prev)(to_prev(j).start)
        pl.when(jnp.logical_and(has_next, core == 0))(to_next(j).start)
        wide = units.astype(jnp.float32)
        plain[HALO : HALO + rows, cols] = wide
        offset4[HALO - 4 : HALO - 4 + rows, cols] = wide

    local[8].wait()

    def first_row(i, t):
        return i * CONV_ROWS + HALO + DILATION * (t - KERNEL // 2)

    def is_own(i, t):
        return first_row(i, t) >= HALO and first_row(i, t) + CONV_ROWS <= HALO + rows

    def add_taps(total, i, cols, chosen):
        for t in chosen:
            row = first_row(i, t)
            source = plain if row % 8 == 0 else offset4
            row -= row % 8
            term = taps[t : t + 1, cols] * source[row : row + CONV_ROWS, cols]
            total = term if total is None else total + term
        return total

    tiles = [
        (i, slice(c * CONV_COLS, (c + 1) * CONV_COLS))
        for c in range(width // CONV_COLS)
        for i in range(rows // CONV_ROWS)
    ]
    for i, cols in tiles:
        conv[i * CONV_ROWS : (i + 1) * CONV_ROWS, cols] = add_taps(
            None, i, cols, [t for t in range(KERNEL) if is_own(i, t)]
        )

    for c in range(width // CONV_COLS):
        half = slice(c * CONV_COLS, (c + 1) * CONV_COLS)
        for j in range(half.start // GATE_COLS, half.stop // GATE_COLS):
            pl.when(has_next)(lambda j=j: to_prev(j).wait_recv())
            pl.when(has_prev)(lambda j=j: to_next(j).wait_recv())
        left = gated[0:HALO, half].astype(jnp.float32)
        right = gated[HALO + rows : 2 * HALO + rows, half].astype(jnp.float32)
        plain[0:HALO, half] = left
        plain[HALO + rows : 2 * HALO + rows, half] = right
        offset4[0 : HALO - 4, half] = left[4:HALO]
        offset4[HALO - 4 + rows : 2 * HALO - 4 + rows, half] = right
        for i in range(rows // CONV_ROWS):
            here = slice(i * CONV_ROWS, (i + 1) * CONV_ROWS)
            conv[here, half] = add_taps(
                conv[here, half], i, half, [t for t in range(KERNEL) if not is_own(i, t)]
            )

    local[9].wait()
    inner = layer_norm(conv[...], inner_gain[...])
    activated = (inner * jax.nn.sigmoid(inner)).astype(jnp.bfloat16)
    local[10].wait()
    leaving = []
    for j in range(gate_chunks):
        cols = slice(j * GATE_COLS, (j + 1) * GATE_COLS)
        result[:, cols] = (
            frames[:, cols].astype(jnp.float32)
            + jnp.dot(activated, shrink[:, cols], preferred_element_type=jnp.float32)
        ).astype(jnp.bfloat16)
        leaving.append(
            pltpu.make_async_copy(result.at[:, cols], out.at[:, cols], out_sem.at[j])
        )
        leaving[j].start()

    for g in range(chunks):
        for part in range(2):
            y_copy(g, part, y_target).wait_send()
            p_copy(g, part, p_target).wait_send()
            pl.when(z_sends)(z_copy(g, part).wait_send)
            pl.when(c_sends)(c_copy(g, part, c_target).wait_send)
    for j in range(gate_chunks):
        pl.when(has_prev)(lambda j=j: to_prev(j).wait_send())
        pl.when(has_next)(lambda j=j: to_next(j).wait_send())
    for copy in leaving:
        copy.wait()


def hand_over(source, target, held, in_sems, out_sems):
    count = in_sems.shape[0]
    part_rows = source.shape[0] // count
    parts = [pl.ds(i * part_rows, part_rows) for i in range(count)]
    inward = [
        pltpu.make_async_copy(source.at[part, :], held.at[part, :], in_sems.at[i])
        for i, part in enumerate(parts)
    ]
    outward = [
        pltpu.make_async_copy(held.at[part, :], target.at[part, :], out_sems.at[i])
        for i, part in enumerate(parts)
    ]
    for copy in inward:
        copy.start()
    for first, second in zip(inward, outward):
        first.wait()
        second.start()
    for copy in outward:
        copy.wait()


def on_device(
    frames_in,
    query_proj,
    key_proj,
    value_proj,
    utterance_lengths,
    bucket_table,
    bucket_bias,
    out_weight,
    norm_gain,
    expand_weight,
    depth_taps,
    inner_gain,
    shrink_weight,
):
    rows, width = frames_in.shape
    att_width = query_proj.shape[1]
    chunks = att_width // CHUNK
    gate_chunks = width // GATE_COLS
    window = SLOTS * rows
    heads_here = CHUNK // (att_width // bucket_bias.shape[1])
    wide_rows = rows + 2 * HALO
    bf16, f32 = jnp.bfloat16, jnp.float32
    anywhere = pl.BlockSpec(memory_space=pl.ANY)
    dma = pltpu.SemaphoreType.DMA
    block_out = pl.pallas_call(
        functools.partial(kernel, lax.axis_size("seq")),
        out_shape=jax.ShapeDtypeStruct((rows, width), bf16),
        in_specs=[anywhere] * 13,
        out_specs=anywhere,
        scratch_shapes=[
            pltpu.SMEM(utterance_lengths.shape, jnp.int32),
            pltpu.VMEM(bucket_table.shape, jnp.int32),
            pltpu.VMEM(bucket_bias.shape[::-1], f32),
            pltpu.VMEM((1, width), f32),
            pltpu.VMEM((1, width), f32),
            pltpu.VMEM((rows, width), bf16),
            pltpu.VMEM((rows, att_width), bf16),
            pltpu.VMEM(out_weight.shape, bf16),
            pltpu.VMEM(expand_weight.shape, bf16),
            pltpu.VMEM(depth_taps.shape, f32),
            pltpu.VMEM(shrink_weight.shape, bf16),
            pltpu.VMEM((chunks, 2, window, CHUNK), bf16),
            pltpu.VMEM((1, window + rows), jnp.int32),
            pltpu.VMEM((chunks, heads_here * rows, window), f32),
            pltpu.VMEM((rows, att_width), bf16),
            pltpu.VMEM((wide_rows, width), bf16),
            pltpu.VMEM((wide_rows, width), f32),
            pltpu.VMEM((wide_rows, width), f32),
            pltpu.VMEM((rows, width), f32),
            pltpu.VMEM((rows, width), bf16),
            pltpu.VMEM((chunks, heads_here * rows, window), bf16),
            dma((11,)),
            dma((chunks, 2)),
            dma((chunks, 2)),
            dma((chunks, 2)),
            dma((chunks, 2)),
            dma((chunks, 2)),
            dma((chunks, 2)),
            dma((chunks, 2)),
            dma((chunks, 2)),
            dma((chunks, 2)),
            dma((2, gate_chunks)),
            dma((2, gate_chunks)),
            dma((gate_chunks,)),
        ],
        compiler_params=pltpu.CompilerParams(
            collective_id=0, has_side_effects=True, vmem_limit_bytes=60 * 1024 * 1024
        ),
    )(
        utterance_lengths,
        bucket_table,
        bucket_bias.T,
        norm_gain.reshape(1, -1),
        inner_gain.reshape(1, -1),
        frames_in,
        query_proj,
        key_proj,
        value_proj,
        out_weight,
        expand_weight,
        depth_taps,
        shrink_weight,
    )
    return pl.pallas_call(
        hand_over,
        out_shape=jax.ShapeDtypeStruct((rows, width), bf16),
        in_specs=[anywhere],
        out_specs=anywhere,
        scratch_shapes=[pltpu.VMEM((rows, width), bf16), dma((4,)), dma((4,))],
        compiler_params=pltpu.CompilerParams(vmem_limit_bytes=60 * 1024 * 1024),
    )(block_out)


def solution(mesh):
    placed = (
        P(("groups", "seq"), None),
        P(("groups", "seq"), None),
        P(("groups", "seq"), None),
        P(("groups", "seq"), None),
        P("groups"),
        P(),
        P(),
        P(),
        P(),
        P(),
        P(),
        P(),
        P(),
    )
    return jax.shard_map(
        on_device, mesh=mesh, in_specs=placed, out_specs=P(("groups", "seq"), None), check_vma=False
    )
```

```python
import functools

import jax
import jax.numpy as jnp
from jax import lax
from jax.experimental import pallas as pl
from jax.experimental.pallas import tpu as pltpu
from jax.sharding import PartitionSpec as P

KERNEL = 31
DILATION = 4
REACH = 2
SLOTS = 2 * REACH + 1
CHUNK = 128
GATE_COLS = 256
HALO = 64
Z_LAG = 4
USE_LAG = 7
CONV_ROWS = 32
CONV_COLS = 512

norm_epsilon = 1e-05
masked_score = -1e30


def layer_norm(values, gain_vec):
    row_mean = jnp.mean(values, axis=-1, keepdims=True)
    centred = values - row_mean
    spread = jnp.mean(centred * centred, axis=-1, keepdims=True)
    return centred * lax.rsqrt(spread + norm_epsilon) * gain_vec


def kernel(
    seq_count,
    lengths_hbm,
    table_hbm,
    bucket_bias_hbm,
    norm_gain_hbm,
    inner_gain_hbm,
    frames_hbm,
    query_hbm,
    key_hbm,
    value_hbm,
    out_w_hbm,
    expand_hbm,
    taps_hbm,
    shrink_hbm,
    out,
    lengths,
    table,
    bucket_bias,
    norm_gain,
    inner_gain,
    frames,
    query,
    out_w,
    expand,
    taps,
    shrink,
    kv,
    table_pad,
    bias,
    attended,
    gated,
    plain,
    offset4,
    conv,
    result,
    weights,
    local_sem,
    own_sem,
    p_send,
    p_recv,
    y_send,
    y_recv,
    z_send,
    z_recv,
    c_send,
    c_recv,
    h_send,
    h_recv,
    out_sem,
):
    rows, width = frames.shape
    att_width = query.shape[1]
    chunks = att_width // CHUNK
    head_width = att_width // bucket_bias.shape[0]
    window = SLOTS * rows
    gate_chunks = width // GATE_COLS

    me = lax.axis_index("seq")
    core = lax.rem(me, 2)
    is_a = lax.rem(me, 4) < 2
    outer = is_a == (core == 0)
    partner = me + 1 - 2 * core
    y_peer = jnp.where(is_a, me + 2, me - 2)
    z_to = jnp.where(is_a, me + 4, me - 4)
    z_from = jnp.where(is_a, me - 4, me + 4)
    beside = jnp.where(core == 0, me - 1, me + 1)
    z_sends = jnp.logical_and(z_to >= 0, z_to < seq_count)
    z_gets = jnp.logical_and(z_from >= 0, z_from < seq_count)
    beside_is = jnp.logical_and(beside >= 0, beside < seq_count)
    c_sends = jnp.logical_or(outer, z_gets)
    c_gets = jnp.logical_or(jnp.logical_not(outer), z_gets)
    y_slot = jnp.where(is_a, 4, 0)
    z_slot = jnp.where(is_a, 0, 4)
    c_slot = jnp.where(core == 0, 1, 3)

    def slot_rows(slot):
        return pl.ds(pl.multiple_of(slot * rows, rows), rows)

    own = []
    for part, source in enumerate((key_hbm, value_hbm)):
        for g in range(chunks):
            own.append(
                pltpu.make_async_copy(
                    source.at[:, pl.ds(g * CHUNK, CHUNK)],
                    kv.at[g, part, pl.ds(REACH * rows, rows), :],
                    own_sem.at[g, part],
                )
            )
    local = [
        pltpu.make_async_copy(source, target, local_sem.at[i])
        for i, (source, target) in enumerate(
            (
                (lengths_hbm, lengths),
                (table_hbm, table),
                (bucket_bias_hbm, bucket_bias),
                (query_hbm, query),
                (frames_hbm, frames),
                (out_w_hbm, out_w),
                (norm_gain_hbm, norm_gain),
                (expand_hbm, expand),
                (taps_hbm, taps),
                (inner_gain_hbm, inner_gain),
                (shrink_hbm, shrink),
            )
        )
    ]

    barrier = pltpu.get_barrier_semaphore()

    def greet(device):
        pl.semaphore_signal(
            barrier, inc=1, device_id={"seq": device}, device_id_type=pl.DeviceIdType.MESH
        )

    greet(partner)
    greet(y_peer)
    pl.when(z_sends)(lambda: greet(z_to))
    pl.when(z_gets)(lambda: greet(z_from))
    pl.when(beside_is)(lambda: greet(beside))
    for copy in local[:4] + own:
        copy.start()
    greetings = (
        2 + z_sends.astype(jnp.int32) + z_gets.astype(jnp.int32) + beside_is.astype(jnp.int32)
    )
    pl.semaphore_wait(barrier, greetings)

    def remote(source, target, send, recv, device):
        return pltpu.make_async_remote_copy(
            src_ref=source,
            dst_ref=target,
            send_sem=send,
            recv_sem=recv,
            device_id={"seq": device},
            device_id_type=pl.DeviceIdType.MESH,
        )

    def own_copy(g, part, slot, send, recv, device):
        source = (key_hbm, value_hbm)[part]
        return remote(
            source.at[:, pl.ds(g * CHUNK, CHUNK)],
            kv.at[g, part, slot_rows(slot), :],
            send.at[g, part],
            recv.at[g, part],
            device,
        )

    def relay(g, part, from_slot, to_slot, send, recv, device):
        return remote(
            kv.at[g, part, slot_rows(from_slot), :],
            kv.at[g, part, slot_rows(to_slot), :],
            send.at[g, part],
            recv.at[g, part],
            device,
        )

    def y_copy(g, part, slot):
        return own_copy(g, part, slot, y_send, y_recv, y_peer)

    def p_copy(g, part, slot):
        return own_copy(g, part, slot, p_send, p_recv, partner)

    y_target = jnp.where(is_a, 0, 4)
    p_target = 2 * core + 1
    p_slot = 3 - 2 * core
    c_target = jnp.where(core == 0, 3, 1)
    c_source = jnp.where(outer, y_slot, z_slot)

    def z_copy(g, part):
        return relay(g, part, y_slot, z_slot, z_send, z_recv, z_to)

    def c_copy(g, part, target):
        return relay(g, part, c_source, target, c_send, c_recv, partner)

    pieces = [(g, part) for part in range(2) for g in range(chunks)]
    for g, part in pieces:
        y_copy(g, part, y_target).start()

    @pl.when(jnp.logical_not(z_gets))
    def _():
        for g in range(chunks):
            kv[g, :, slot_rows(z_slot), :] = jnp.zeros((2, rows, CHUNK), kv.dtype)

    @pl.when(jnp.logical_not(c_gets))
    def _():
        for g in range(chunks):
            kv[g, :, slot_rows(c_slot), :] = jnp.zeros((2, rows, CHUNK), kv.dtype)

    zero_halo = jnp.zeros((HALO, width), gated.dtype)

    @pl.when(me == 0)
    def _():
        gated[0:HALO, :] = zero_halo

    @pl.when(me == seq_count - 1)
    def _():
        gated[HALO + rows : 2 * HALO + rows, :] = zero_halo

    for copy in local[:3]:
        copy.wait()

    query_at = me * rows + lax.broadcasted_iota(jnp.int32, (rows, 1), 0)
    key_at = (me - REACH) * rows + lax.broadcasted_iota(jnp.int32, (1, window), 1)

    def count(u, state):
        bound, query_seg, key_seg = state
        bound = bound + lengths[u]
        return (
            bound,
            query_seg + (query_at >= bound).astype(jnp.int32),
            key_seg + (key_at >= bound).astype(jnp.int32),
        )

    utterances = lengths.shape[0]
    _, query_seg, key_seg = lax.fori_loop(
        0,
        utterances,
        count,
        (jnp.int32(0), jnp.zeros((rows, 1), jnp.int32), jnp.zeros((1, window), jnp.int32)),
        unroll=utterances <= 32,
    )
    key_seg = jnp.where(key_at < 0, -1, key_seg)

    line_length = table.shape[0]
    padded_length = window + rows
    table_pad[...] = jnp.zeros_like(table_pad)
    table_pad[:, 0:line_length] = table[...].reshape(1, line_length)
    buckets = bucket_bias.shape[1]
    hits = (
        lax.broadcasted_iota(jnp.int32, (buckets, padded_length), 0) == table_pad[...]
    ).astype(jnp.float32)
    bias_line = jnp.dot(
        bucket_bias[...],
        hits,
        precision=lax.Precision.HIGHEST,
        preferred_element_type=jnp.float32,
    )
    heads_here = CHUNK // head_width

    def make_bias(g):
        same = query_seg == key_seg
        for h in range(heads_here):
            head = g * heads_here + h
            line = jnp.broadcast_to(bias_line[head : head + 1, :], (8, padded_length))
            skewed = pltpu.roll(line, padded_length - (rows - 1), 1, stride=1, stride_axis=0)
            for first in range(0, rows, 8):
                block = skewed if first == 0 else pltpu.roll(skewed, first, 1)
                bias[g, h * rows + first : h * rows + first + 8, :] = jnp.where(
                    same[first : first + 8], block[:, :window], masked_score
                )

    head_of_lane = lax.broadcasted_iota(jnp.int32, (rows, CHUNK), 1) // head_width

    def arrive(g, part):
        own[part * chunks + g].wait()
        p_copy(g, part, p_slot).wait_recv()
        pl.when(c_gets)(c_copy(g, part, c_slot).wait_recv)

    def weigh(g):
        chunk_query = query[:, g * CHUNK : (g + 1) * CHUNK]
        stacked = jnp.concatenate(
            [
                jnp.where(head_of_lane == h, chunk_query, jnp.zeros_like(chunk_query))
                for h in range(heads_here)
            ],
            axis=0,
        )
        scores = lax.dot_general(
            stacked, kv[g, 0], (((1,), (1,)), ((), ())), preferred_element_type=jnp.float32
        )
        scores = scores * (head_width**-0.5) + bias[g]
        top = jnp.max(scores, axis=1, keepdims=True)
        weights[g] = jnp.exp(scores - top).astype(jnp.bfloat16)

    def attend(g):
        values_and_ones = jnp.concatenate([kv[g, 1], jnp.ones_like(kv[g, 1])], axis=1)
        weighted = jnp.dot(weights[g], values_and_ones, preferred_element_type=jnp.float32)
        normal = (weighted[:, :CHUNK] / weighted[:, CHUNK:]).astype(jnp.bfloat16)
        chosen = normal[0:rows]
        for h in range(1, heads_here):
            chosen = jnp.where(head_of_lane == h, normal[h * rows : (h + 1) * rows], chosen)
        attended[:, g * CHUNK : (g + 1) * CHUNK] = chosen

    def use(g, part):
        arrive(g, part)
        (weigh, attend)[part](g)

    def pass_y(g, part):
        y_copy(g, part, y_slot).wait_recv()
        pl.when(z_sends)(z_copy(g, part).start)
        pl.when(outer)(c_copy(g, part, c_target).start)

    def pass_z(g, part):
        @pl.when(z_gets)
        def _():
            relay(g, part, y_slot, z_slot, z_send, z_recv, z_to).wait_recv()

        @pl.when(jnp.logical_and(z_gets, jnp.logical_not(outer)))
        def _():
            c_copy(g, part, c_target).start()

    half_att = att_width // 2

    def project(half):
        part = slice(half * half_att, (half + 1) * half_att)
        return jnp.dot(attended[:, part], out_w[part, :], preferred_element_type=jnp.float32)

    local[3].wait()
    make_bias(0)
    make_bias(1)
    count_of = len(pieces)
    for step in range(count_of + USE_LAG):
        if step < count_of:
            pass_y(*pieces[step])
            p_copy(*pieces[step], p_target).start()
        for copy in local[4 + step : 5 + step]:
            copy.start()
        if 0 <= step - Z_LAG < count_of:
            pass_z(*pieces[step - Z_LAG])
        if step + 2 < chunks:
            make_bias(step + 2)
        if step == count_of + USE_LAG - 1:
            for copy in local[4:7]:
                copy.wait()
            conv[...] = frames[...].astype(jnp.float32) + project(0)
        if step >= USE_LAG:
            use(*pieces[step - USE_LAG])

    mid = (conv[...] + project(1)).astype(jnp.bfloat16)
    frames[...] = mid
    normed = layer_norm(mid.astype(jnp.float32), norm_gain[...]).astype(jnp.bfloat16)
    local[7].wait()

    def to_prev(j):
        cols = pl.ds(j * GATE_COLS, GATE_COLS)
        return remote(
            gated.at[pl.ds(HALO, HALO), cols],
            gated.at[pl.ds(HALO + rows, HALO), cols],
            h_send.at[0, j],
            h_recv.at[0, j],
            me - 1,
        )

    def to_next(j):
        cols = pl.ds(j * GATE_COLS, GATE_COLS)
        return remote(
            gated.at[pl.ds(rows, HALO), cols],
            gated.at[pl.ds(0, HALO), cols],
            h_send.at[1, j],
            h_recv.at[1, j],
            me + 1,
        )

    has_prev = me > 0
    has_next = me < seq_count - 1
    for j in range(gate_chunks):
        first = j * GATE_COLS
        cols = slice(first, first + GATE_COLS)
        linear = jnp.dot(normed, expand[:, cols], preferred_element_type=jnp.float32)
        gate = jnp.dot(
            normed,
            expand[:, width + first : width + first + GATE_COLS],
            preferred_element_type=jnp.float32,
        )
        units = (linear * jax.nn.sigmoid(gate)).astype(jnp.bfloat16)
        gated[HALO : HALO + rows, cols] = units
        pl.when(jnp.logical_and(has_next, core == 1))(to_next(j).start)
        pl.when(has_prev)(to_prev(j).start)
        pl.when(jnp.logical_and(has_next, core == 0))(to_next(j).start)
        wide = units.astype(jnp.float32)
        plain[HALO : HALO + rows, cols] = wide
        offset4[HALO - 4 : HALO - 4 + rows, cols] = wide

    local[8].wait()

    def first_row(i, t):
        return i * CONV_ROWS + HALO + DILATION * (t - KERNEL // 2)

    def is_own(i, t):
        return first_row(i, t) >= HALO and first_row(i, t) + CONV_ROWS <= HALO + rows

    def add_taps(total, i, cols, chosen):
        for t in chosen:
            row = first_row(i, t)
            source = plain if row % 8 == 0 else offset4
            row -= row % 8
            term = taps[t : t + 1, cols] * source[row : row + CONV_ROWS, cols]
            total = term if total is None else total + term
        return total

    tiles = [
        (i, slice(c * CONV_COLS, (c + 1) * CONV_COLS))
        for c in range(width // CONV_COLS)
        for i in range(rows // CONV_ROWS)
    ]
    for i, cols in tiles:
        conv[i * CONV_ROWS : (i + 1) * CONV_ROWS, cols] = add_taps(
            None, i, cols, [t for t in range(KERNEL) if is_own(i, t)]
        )

    for c in range(width // CONV_COLS):
        half = slice(c * CONV_COLS, (c + 1) * CONV_COLS)
        for j in range(half.start // GATE_COLS, half.stop // GATE_COLS):
            pl.when(has_next)(lambda j=j: to_prev(j).wait_recv())
            pl.when(has_prev)(lambda j=j: to_next(j).wait_recv())
        left = gated[0:HALO, half].astype(jnp.float32)
        right = gated[HALO + rows : 2 * HALO + rows, half].astype(jnp.float32)
        plain[0:HALO, half] = left
        plain[HALO + rows : 2 * HALO + rows, half] = right
        offset4[0 : HALO - 4, half] = left[4:HALO]
        offset4[HALO - 4 + rows : 2 * HALO - 4 + rows, half] = right
        for i in range(rows // CONV_ROWS):
            here = slice(i * CONV_ROWS, (i + 1) * CONV_ROWS)
            conv[here, half] = add_taps(
                conv[here, half], i, half, [t for t in range(KERNEL) if not is_own(i, t)]
            )

    local[9].wait()
    inner = layer_norm(conv[...], inner_gain[...])
    activated = (inner * jax.nn.sigmoid(inner)).astype(jnp.bfloat16)
    local[10].wait()
    leaving = []
    for j in range(gate_chunks):
        cols = slice(j * GATE_COLS, (j + 1) * GATE_COLS)
        result[:, cols] = (
            frames[:, cols].astype(jnp.float32)
            + jnp.dot(activated, shrink[:, cols], preferred_element_type=jnp.float32)
        ).astype(jnp.bfloat16)
        leaving.append(
            pltpu.make_async_copy(result.at[:, cols], out.at[:, cols], out_sem.at[j])
        )
        leaving[j].start()

    for g in range(chunks):
        for part in range(2):
            y_copy(g, part, y_target).wait_send()
            p_copy(g, part, p_target).wait_send()
            pl.when(z_sends)(z_copy(g, part).wait_send)
            pl.when(c_sends)(c_copy(g, part, c_target).wait_send)
    for j in range(gate_chunks):
        pl.when(has_prev)(lambda j=j: to_prev(j).wait_send())
        pl.when(has_next)(lambda j=j: to_next(j).wait_send())
    for copy in leaving:
        copy.wait()


def hand_over(source, target, held, in_sems, out_sems):
    count = in_sems.shape[0]
    part_rows = source.shape[0] // count
    parts = [pl.ds(i * part_rows, part_rows) for i in range(count)]
    inward = [
        pltpu.make_async_copy(source.at[part, :], held.at[part, :], in_sems.at[i])
        for i, part in enumerate(parts)
    ]
    outward = [
        pltpu.make_async_copy(held.at[part, :], target.at[part, :], out_sems.at[i])
        for i, part in enumerate(parts)
    ]
    for copy in inward:
        copy.start()
    for first, second in zip(inward, outward):
        first.wait()
        second.start()
    for copy in outward:
        copy.wait()


def on_device(
    frames_in,
    query_proj,
    key_proj,
    value_proj,
    utterance_lengths,
    bucket_table,
    bucket_bias,
    out_weight,
    norm_gain,
    expand_weight,
    depth_taps,
    inner_gain,
    shrink_weight,
):
    rows, width = frames_in.shape
    att_width = query_proj.shape[1]
    chunks = att_width // CHUNK
    gate_chunks = width // GATE_COLS
    window = SLOTS * rows
    heads_here = CHUNK // (att_width // bucket_bias.shape[1])
    wide_rows = rows + 2 * HALO
    bf16, f32 = jnp.bfloat16, jnp.float32
    anywhere = pl.BlockSpec(memory_space=pl.ANY)
    dma = pltpu.SemaphoreType.DMA
    block_out = pl.pallas_call(
        functools.partial(kernel, lax.axis_size("seq")),
        out_shape=jax.ShapeDtypeStruct((rows, width), bf16),
        in_specs=[anywhere] * 13,
        out_specs=anywhere,
        scratch_shapes=[
            pltpu.SMEM(utterance_lengths.shape, jnp.int32),
            pltpu.VMEM(bucket_table.shape, jnp.int32),
            pltpu.VMEM(bucket_bias.shape[::-1], f32),
            pltpu.VMEM((1, width), f32),
            pltpu.VMEM((1, width), f32),
            pltpu.VMEM((rows, width), bf16),
            pltpu.VMEM((rows, att_width), bf16),
            pltpu.VMEM(out_weight.shape, bf16),
            pltpu.VMEM(expand_weight.shape, bf16),
            pltpu.VMEM(depth_taps.shape, f32),
            pltpu.VMEM(shrink_weight.shape, bf16),
            pltpu.VMEM((chunks, 2, window, CHUNK), bf16),
            pltpu.VMEM((1, window + rows), jnp.int32),
            pltpu.VMEM((chunks, heads_here * rows, window), f32),
            pltpu.VMEM((rows, att_width), bf16),
            pltpu.VMEM((wide_rows, width), bf16),
            pltpu.VMEM((wide_rows, width), f32),
            pltpu.VMEM((wide_rows, width), f32),
            pltpu.VMEM((rows, width), f32),
            pltpu.VMEM((rows, width), bf16),
            pltpu.VMEM((chunks, heads_here * rows, window), bf16),
            dma((11,)),
            dma((chunks, 2)),
            dma((chunks, 2)),
            dma((chunks, 2)),
            dma((chunks, 2)),
            dma((chunks, 2)),
            dma((chunks, 2)),
            dma((chunks, 2)),
            dma((chunks, 2)),
            dma((chunks, 2)),
            dma((2, gate_chunks)),
            dma((2, gate_chunks)),
            dma((gate_chunks,)),
        ],
        compiler_params=pltpu.CompilerParams(
            collective_id=0, has_side_effects=True, vmem_limit_bytes=60 * 1024 * 1024
        ),
    )(
        utterance_lengths,
        bucket_table,
        bucket_bias.T,
        norm_gain.reshape(1, -1),
        inner_gain.reshape(1, -1),
        frames_in,
        query_proj,
        key_proj,
        value_proj,
        out_weight,
        expand_weight,
        depth_taps,
        shrink_weight,
    )
    return pl.pallas_call(
        hand_over,
        out_shape=jax.ShapeDtypeStruct((rows, width), bf16),
        in_specs=[anywhere],
        out_specs=anywhere,
        scratch_shapes=[pltpu.VMEM((rows, width), bf16), dma((4,)), dma((4,))],
        compiler_params=pltpu.CompilerParams(vmem_limit_bytes=60 * 1024 * 1024),
    )(block_out)


def solution(mesh):
    placed = (
        P(("groups", "seq"), None),
        P(("groups", "seq"), None),
        P(("groups", "seq"), None),
        P(("groups", "seq"), None),
        P("groups"),
        P(),
        P(),
        P(),
        P(),
        P(),
        P(),
        P(),
        P(),
    )
    return jax.shard_map(
        on_device, mesh=mesh, in_specs=placed, out_specs=P(("groups", "seq"), None), check_vma=False
    )
```

```python
import functools

import jax
import jax.numpy as jnp
from jax import lax
from jax.experimental import pallas as pl
from jax.experimental.pallas import tpu as pltpu
from jax.sharding import PartitionSpec as P

KERNEL = 31
DILATION = 4
REACH = 2
SLOTS = 2 * REACH + 1
CHUNK = 128
GATE_COLS = 256
HALO = 64
Z_LAG = 4
USE_LAG = 6
CONV_ROWS = 32
CONV_COLS = 512

norm_epsilon = 1e-05
masked_score = -1e30


def layer_norm(values, gain_vec):
    row_mean = jnp.mean(values, axis=-1, keepdims=True)
    centred = values - row_mean
    spread = jnp.mean(centred * centred, axis=-1, keepdims=True)
    return centred * lax.rsqrt(spread + norm_epsilon) * gain_vec


def kernel(
    seq_count,
    lengths_hbm,
    table_hbm,
    bucket_bias_hbm,
    norm_gain_hbm,
    inner_gain_hbm,
    frames_hbm,
    query_hbm,
    key_hbm,
    value_hbm,
    out_w_hbm,
    expand_hbm,
    taps_hbm,
    shrink_hbm,
    out,
    lengths,
    table,
    bucket_bias,
    norm_gain,
    inner_gain,
    frames,
    query,
    out_w,
    expand,
    taps,
    shrink,
    kv,
    table_pad,
    bias,
    attended,
    gated,
    plain,
    offset4,
    conv,
    result,
    weights,
    local_sem,
    own_sem,
    p_send,
    p_recv,
    y_send,
    y_recv,
    z_send,
    z_recv,
    c_send,
    c_recv,
    h_send,
    h_recv,
    out_sem,
):
    rows, width = frames.shape
    att_width = query.shape[1]
    chunks = att_width // CHUNK
    head_width = att_width // bucket_bias.shape[0]
    window = SLOTS * rows
    gate_chunks = width // GATE_COLS

    me = lax.axis_index("seq")
    core = lax.rem(me, 2)
    is_a = lax.rem(me, 4) < 2
    outer = is_a == (core == 0)
    partner = me + 1 - 2 * core
    y_peer = jnp.where(is_a, me + 2, me - 2)
    z_to = jnp.where(is_a, me + 4, me - 4)
    z_from = jnp.where(is_a, me - 4, me + 4)
    beside = jnp.where(core == 0, me - 1, me + 1)
    z_sends = jnp.logical_and(z_to >= 0, z_to < seq_count)
    z_gets = jnp.logical_and(z_from >= 0, z_from < seq_count)
    beside_is = jnp.logical_and(beside >= 0, beside < seq_count)
    c_sends = jnp.logical_or(outer, z_gets)
    c_gets = jnp.logical_or(jnp.logical_not(outer), z_gets)
    y_slot = jnp.where(is_a, 4, 0)
    z_slot = jnp.where(is_a, 0, 4)
    c_slot = jnp.where(core == 0, 1, 3)

    def slot_rows(slot):
        return pl.ds(pl.multiple_of(slot * rows, rows), rows)

    own = []
    for part, source in enumerate((key_hbm, value_hbm)):
        for g in range(chunks):
            own.append(
                pltpu.make_async_copy(
                    source.at[:, pl.ds(g * CHUNK, CHUNK)],
                    kv.at[g, part, pl.ds(REACH * rows, rows), :],
                    own_sem.at[g, part],
                )
            )
    local = [
        pltpu.make_async_copy(source, target, local_sem.at[i])
        for i, (source, target) in enumerate(
            (
                (lengths_hbm, lengths),
                (table_hbm, table),
                (bucket_bias_hbm, bucket_bias),
                (query_hbm, query),
                (frames_hbm, frames),
                (out_w_hbm, out_w),
                (norm_gain_hbm, norm_gain),
                (expand_hbm, expand),
                (taps_hbm, taps),
                (inner_gain_hbm, inner_gain),
                (shrink_hbm, shrink),
            )
        )
    ]

    barrier = pltpu.get_barrier_semaphore()

    def greet(device):
        pl.semaphore_signal(
            barrier, inc=1, device_id={"seq": device}, device_id_type=pl.DeviceIdType.MESH
        )

    greet(partner)
    greet(y_peer)
    pl.when(z_sends)(lambda: greet(z_to))
    pl.when(z_gets)(lambda: greet(z_from))
    pl.when(beside_is)(lambda: greet(beside))
    for copy in local[:4] + own:
        copy.start()
    greetings = (
        2 + z_sends.astype(jnp.int32) + z_gets.astype(jnp.int32) + beside_is.astype(jnp.int32)
    )
    pl.semaphore_wait(barrier, greetings)

    def remote(source, target, send, recv, device):
        return pltpu.make_async_remote_copy(
            src_ref=source,
            dst_ref=target,
            send_sem=send,
            recv_sem=recv,
            device_id={"seq": device},
            device_id_type=pl.DeviceIdType.MESH,
        )

    def own_copy(g, part, slot, send, recv, device):
        source = (key_hbm, value_hbm)[part]
        return remote(
            source.at[:, pl.ds(g * CHUNK, CHUNK)],
            kv.at[g, part, slot_rows(slot), :],
            send.at[g, part],
            recv.at[g, part],
            device,
        )

    def relay(g, part, from_slot, to_slot, send, recv, device):
        return remote(
            kv.at[g, part, slot_rows(from_slot), :],
            kv.at[g, part, slot_rows(to_slot), :],
            send.at[g, part],
            recv.at[g, part],
            device,
        )

    def y_copy(g, part, slot):
        return own_copy(g, part, slot, y_send, y_recv, y_peer)

    def p_copy(g, part, slot):
        return own_copy(g, part, slot, p_send, p_recv, partner)

    y_target = jnp.where(is_a, 0, 4)
    p_target = 2 * core + 1
    p_slot = 3 - 2 * core
    c_target = jnp.where(core == 0, 3, 1)
    c_source = jnp.where(outer, y_slot, z_slot)

    def z_copy(g, part):
        return relay(g, part, y_slot, z_slot, z_send, z_recv, z_to)

    def c_copy(g, part, target):
        return relay(g, part, c_source, target, c_send, c_recv, partner)

    pieces = [(g, part) for part in range(2) for g in range(chunks)]

    def send_own(g, part):
        y_copy(g, part, y_target).start()
        p_copy(g, part, p_target).start()

    for piece in pieces:
        send_own(*piece)

    @pl.when(jnp.logical_not(z_gets))
    def _():
        for g in range(chunks):
            kv[g, :, slot_rows(z_slot), :] = jnp.zeros((2, rows, CHUNK), kv.dtype)

    @pl.when(jnp.logical_not(c_gets))
    def _():
        for g in range(chunks):
            kv[g, :, slot_rows(c_slot), :] = jnp.zeros((2, rows, CHUNK), kv.dtype)

    zero_halo = jnp.zeros((HALO, width), gated.dtype)

    @pl.when(me == 0)
    def _():
        gated[0:HALO, :] = zero_halo

    @pl.when(me == seq_count - 1)
    def _():
        gated[HALO + rows : 2 * HALO + rows, :] = zero_halo

    for copy in local[:3]:
        copy.wait()

    query_at = me * rows + lax.broadcasted_iota(jnp.int32, (rows, 1), 0)
    key_at = (me - REACH) * rows + lax.broadcasted_iota(jnp.int32, (1, window), 1)

    def count(u, state):
        bound, query_seg, key_seg = state
        bound = bound + lengths[u]
        return (
            bound,
            query_seg + (query_at >= bound).astype(jnp.int32),
            key_seg + (key_at >= bound).astype(jnp.int32),
        )

    utterances = lengths.shape[0]
    _, query_seg, key_seg = lax.fori_loop(
        0,
        utterances,
        count,
        (jnp.int32(0), jnp.zeros((rows, 1), jnp.int32), jnp.zeros((1, window), jnp.int32)),
        unroll=utterances <= 32,
    )
    key_seg = jnp.where(key_at < 0, -1, key_seg)

    line_length = table.shape[0]
    padded_length = window + rows
    table_pad[...] = jnp.zeros_like(table_pad)
    table_pad[:, 0:line_length] = table[...].reshape(1, line_length)
    buckets = bucket_bias.shape[1]
    hits = (
        lax.broadcasted_iota(jnp.int32, (buckets, padded_length), 0) == table_pad[...]
    ).astype(jnp.float32)
    bias_line = jnp.dot(
        bucket_bias[...],
        hits,
        precision=lax.Precision.HIGHEST,
        preferred_element_type=jnp.float32,
    )
    heads_here = CHUNK // head_width

    def make_bias(g):
        same = query_seg == key_seg
        for h in range(heads_here):
            head = g * heads_here + h
            line = jnp.broadcast_to(bias_line[head : head + 1, :], (8, padded_length))
            skewed = pltpu.roll(line, padded_length - (rows - 1), 1, stride=1, stride_axis=0)
            for first in range(0, rows, 8):
                block = skewed if first == 0 else pltpu.roll(skewed, first, 1)
                bias[g, h * rows + first : h * rows + first + 8, :] = jnp.where(
                    same[first : first + 8], block[:, :window], masked_score
                )

    head_of_lane = lax.broadcasted_iota(jnp.int32, (rows, CHUNK), 1) // head_width

    def arrive(g, part):
        own[part * chunks + g].wait()
        p_copy(g, part, p_slot).wait_recv()
        pl.when(c_gets)(c_copy(g, part, c_slot).wait_recv)

    def weigh(g):
        chunk_query = query[:, g * CHUNK : (g + 1) * CHUNK]
        stacked = jnp.concatenate(
            [
                jnp.where(head_of_lane == h, chunk_query, jnp.zeros_like(chunk_query))
                for h in range(heads_here)
            ],
            axis=0,
        )
        scores = lax.dot_general(
            stacked, kv[g, 0], (((1,), (1,)), ((), ())), preferred_element_type=jnp.float32
        )
        scores = scores * (head_width**-0.5) + bias[g]
        top = jnp.max(scores, axis=1, keepdims=True)
        weights[g] = jnp.exp(scores - top).astype(jnp.bfloat16)

    def attend(g):
        values_and_ones = jnp.concatenate([kv[g, 1], jnp.ones_like(kv[g, 1])], axis=1)
        weighted = jnp.dot(weights[g], values_and_ones, preferred_element_type=jnp.float32)
        normal = (weighted[:, :CHUNK] / weighted[:, CHUNK:]).astype(jnp.bfloat16)
        chosen = normal[0:rows]
        for h in range(1, heads_here):
            chosen = jnp.where(head_of_lane == h, normal[h * rows : (h + 1) * rows], chosen)
        attended[:, g * CHUNK : (g + 1) * CHUNK] = chosen

    def use(g, part):
        arrive(g, part)
        (weigh, attend)[part](g)

    def pass_y(g, part):
        y_copy(g, part, y_slot).wait_recv()
        pl.when(z_sends)(z_copy(g, part).start)
        pl.when(outer)(c_copy(g, part, c_target).start)

    def pass_z(g, part):
        @pl.when(z_gets)
        def _():
            relay(g, part, y_slot, z_slot, z_send, z_recv, z_to).wait_recv()

        @pl.when(jnp.logical_and(z_gets, jnp.logical_not(outer)))
        def _():
            c_copy(g, part, c_target).start()

    half_att = att_width // 2

    def project(half):
        part = slice(half * half_att, (half + 1) * half_att)
        return jnp.dot(attended[:, part], out_w[part, :], preferred_element_type=jnp.float32)

    local[3].wait()
    make_bias(0)
    make_bias(1)
    count_of = len(pieces)
    for step in range(count_of + USE_LAG):
        if step < count_of:
            pass_y(*pieces[step])
        for copy in local[4 + step : 5 + step]:
            copy.start()
        if 0 <= step - Z_LAG < count_of:
            pass_z(*pieces[step - Z_LAG])
        if step + 2 < chunks:
            make_bias(step + 2)
        if step == count_of + USE_LAG - 1:
            for copy in local[4:7]:
                copy.wait()
            conv[...] = frames[...].astype(jnp.float32) + project(0)
        if step >= USE_LAG:
            use(*pieces[step - USE_LAG])

    mid = (conv[...] + project(1)).astype(jnp.bfloat16)
    frames[...] = mid
    normed = layer_norm(mid.astype(jnp.float32), norm_gain[...]).astype(jnp.bfloat16)
    local[7].wait()

    def to_prev(j):
        cols = pl.ds(j * GATE_COLS, GATE_COLS)
        return remote(
            gated.at[pl.ds(HALO, HALO), cols],
            gated.at[pl.ds(HALO + rows, HALO), cols],
            h_send.at[0, j],
            h_recv.at[0, j],
            me - 1,
        )

    def to_next(j):
        cols = pl.ds(j * GATE_COLS, GATE_COLS)
        return remote(
            gated.at[pl.ds(rows, HALO), cols],
            gated.at[pl.ds(0, HALO), cols],
            h_send.at[1, j],
            h_recv.at[1, j],
            me + 1,
        )

    has_prev = me > 0
    has_next = me < seq_count - 1
    for j in range(gate_chunks):
        first = j * GATE_COLS
        cols = slice(first, first + GATE_COLS)
        linear = jnp.dot(normed, expand[:, cols], preferred_element_type=jnp.float32)
        gate = jnp.dot(
            normed,
            expand[:, width + first : width + first + GATE_COLS],
            preferred_element_type=jnp.float32,
        )
        units = (linear * jax.nn.sigmoid(gate)).astype(jnp.bfloat16)
        gated[HALO : HALO + rows, cols] = units
        pl.when(jnp.logical_and(has_next, core == 1))(to_next(j).start)
        pl.when(has_prev)(to_prev(j).start)
        pl.when(jnp.logical_and(has_next, core == 0))(to_next(j).start)
        wide = units.astype(jnp.float32)
        plain[HALO : HALO + rows, cols] = wide
        offset4[HALO - 4 : HALO - 4 + rows, cols] = wide

    local[8].wait()

    def first_row(i, t):
        return i * CONV_ROWS + HALO + DILATION * (t - KERNEL // 2)

    def is_own(i, t):
        return first_row(i, t) >= HALO and first_row(i, t) + CONV_ROWS <= HALO + rows

    def add_taps(total, i, cols, chosen):
        for t in chosen:
            row = first_row(i, t)
            source = plain if row % 8 == 0 else offset4
            row -= row % 8
            term = taps[t : t + 1, cols] * source[row : row + CONV_ROWS, cols]
            total = term if total is None else total + term
        return total

    tiles = [
        (i, slice(c * CONV_COLS, (c + 1) * CONV_COLS))
        for c in range(width // CONV_COLS)
        for i in range(rows // CONV_ROWS)
    ]
    for i, cols in tiles:
        conv[i * CONV_ROWS : (i + 1) * CONV_ROWS, cols] = add_taps(
            None, i, cols, [t for t in range(KERNEL) if is_own(i, t)]
        )

    for c in range(width // CONV_COLS):
        half = slice(c * CONV_COLS, (c + 1) * CONV_COLS)
        for j in range(half.start // GATE_COLS, half.stop // GATE_COLS):
            pl.when(has_next)(lambda j=j: to_prev(j).wait_recv())
            pl.when(has_prev)(lambda j=j: to_next(j).wait_recv())
        left = gated[0:HALO, half].astype(jnp.float32)
        right = gated[HALO + rows : 2 * HALO + rows, half].astype(jnp.float32)
        plain[0:HALO, half] = left
        plain[HALO + rows : 2 * HALO + rows, half] = right
        offset4[0 : HALO - 4, half] = left[4:HALO]
        offset4[HALO - 4 + rows : 2 * HALO - 4 + rows, half] = right
        for i in range(rows // CONV_ROWS):
            here = slice(i * CONV_ROWS, (i + 1) * CONV_ROWS)
            conv[here, half] = add_taps(
                conv[here, half], i, half, [t for t in range(KERNEL) if not is_own(i, t)]
            )

    local[9].wait()
    inner = layer_norm(conv[...], inner_gain[...])
    activated = (inner * jax.nn.sigmoid(inner)).astype(jnp.bfloat16)
    local[10].wait()
    leaving = []
    for j in range(gate_chunks):
        cols = slice(j * GATE_COLS, (j + 1) * GATE_COLS)
        result[:, cols] = (
            frames[:, cols].astype(jnp.float32)
            + jnp.dot(activated, shrink[:, cols], preferred_element_type=jnp.float32)
        ).astype(jnp.bfloat16)
        leaving.append(
            pltpu.make_async_copy(result.at[:, cols], out.at[:, cols], out_sem.at[j])
        )
        leaving[j].start()

    for g in range(chunks):
        for part in range(2):
            y_copy(g, part, y_target).wait_send()
            p_copy(g, part, p_target).wait_send()
            pl.when(z_sends)(z_copy(g, part).wait_send)
            pl.when(c_sends)(c_copy(g, part, c_target).wait_send)
    for j in range(gate_chunks):
        pl.when(has_prev)(lambda j=j: to_prev(j).wait_send())
        pl.when(has_next)(lambda j=j: to_next(j).wait_send())
    for copy in leaving:
        copy.wait()


def hand_over(source, target, held, in_sems, out_sems):
    count = in_sems.shape[0]
    part_rows = source.shape[0] // count
    parts = [pl.ds(i * part_rows, part_rows) for i in range(count)]
    inward = [
        pltpu.make_async_copy(source.at[part, :], held.at[part, :], in_sems.at[i])
        for i, part in enumerate(parts)
    ]
    outward = [
        pltpu.make_async_copy(held.at[part, :], target.at[part, :], out_sems.at[i])
        for i, part in enumerate(parts)
    ]
    for copy in inward:
        copy.start()
    for first, second in zip(inward, outward):
        first.wait()
        second.start()
    for copy in outward:
        copy.wait()


def on_device(
    frames_in,
    query_proj,
    key_proj,
    value_proj,
    utterance_lengths,
    bucket_table,
    bucket_bias,
    out_weight,
    norm_gain,
    expand_weight,
    depth_taps,
    inner_gain,
    shrink_weight,
):
    rows, width = frames_in.shape
    att_width = query_proj.shape[1]
    chunks = att_width // CHUNK
    gate_chunks = width // GATE_COLS
    window = SLOTS * rows
    heads_here = CHUNK // (att_width // bucket_bias.shape[1])
    wide_rows = rows + 2 * HALO
    bf16, f32 = jnp.bfloat16, jnp.float32
    anywhere = pl.BlockSpec(memory_space=pl.ANY)
    dma = pltpu.SemaphoreType.DMA
    block_out = pl.pallas_call(
        functools.partial(kernel, lax.axis_size("seq")),
        out_shape=jax.ShapeDtypeStruct((rows, width), bf16),
        in_specs=[anywhere] * 13,
        out_specs=anywhere,
        scratch_shapes=[
            pltpu.SMEM(utterance_lengths.shape, jnp.int32),
            pltpu.VMEM(bucket_table.shape, jnp.int32),
            pltpu.VMEM(bucket_bias.shape[::-1], f32),
            pltpu.VMEM((1, width), f32),
            pltpu.VMEM((1, width), f32),
            pltpu.VMEM((rows, width), bf16),
            pltpu.VMEM((rows, att_width), bf16),
            pltpu.VMEM(out_weight.shape, bf16),
            pltpu.VMEM(expand_weight.shape, bf16),
            pltpu.VMEM(depth_taps.shape, f32),
            pltpu.VMEM(shrink_weight.shape, bf16),
            pltpu.VMEM((chunks, 2, window, CHUNK), bf16),
            pltpu.VMEM((1, window + rows), jnp.int32),
            pltpu.VMEM((chunks, heads_here * rows, window), f32),
            pltpu.VMEM((rows, att_width), bf16),
            pltpu.VMEM((wide_rows, width), bf16),
            pltpu.VMEM((wide_rows, width), f32),
            pltpu.VMEM((wide_rows, width), f32),
            pltpu.VMEM((rows, width), f32),
            pltpu.VMEM((rows, width), bf16),
            pltpu.VMEM((chunks, heads_here * rows, window), bf16),
            dma((11,)),
            dma((chunks, 2)),
            dma((chunks, 2)),
            dma((chunks, 2)),
            dma((chunks, 2)),
            dma((chunks, 2)),
            dma((chunks, 2)),
            dma((chunks, 2)),
            dma((chunks, 2)),
            dma((chunks, 2)),
            dma((2, gate_chunks)),
            dma((2, gate_chunks)),
            dma((gate_chunks,)),
        ],
        compiler_params=pltpu.CompilerParams(
            collective_id=0, has_side_effects=True, vmem_limit_bytes=60 * 1024 * 1024
        ),
    )(
        utterance_lengths,
        bucket_table,
        bucket_bias.T,
        norm_gain.reshape(1, -1),
        inner_gain.reshape(1, -1),
        frames_in,
        query_proj,
        key_proj,
        value_proj,
        out_weight,
        expand_weight,
        depth_taps,
        shrink_weight,
    )
    return pl.pallas_call(
        hand_over,
        out_shape=jax.ShapeDtypeStruct((rows, width), bf16),
        in_specs=[anywhere],
        out_specs=anywhere,
        scratch_shapes=[pltpu.VMEM((rows, width), bf16), dma((4,)), dma((4,))],
        compiler_params=pltpu.CompilerParams(vmem_limit_bytes=60 * 1024 * 1024),
    )(block_out)


def solution(mesh):
    placed = (
        P(("groups", "seq"), None),
        P(("groups", "seq"), None),
        P(("groups", "seq"), None),
        P(("groups", "seq"), None),
        P("groups"),
        P(),
        P(),
        P(),
        P(),
        P(),
        P(),
        P(),
        P(),
    )
    return jax.shard_map(
        on_device, mesh=mesh, in_specs=placed, out_specs=P(("groups", "seq"), None), check_vma=False
    )
```
